256 devices in a mesh: tok: 64 (over z, y, core), feat: 4 (over x).
Axes of the slice: x: 4, y: 4, z: 8, core: 2. Of those that a mesh axis runs over, the one named last changes fastest.
Arguments:
- doc_in: bfloat16 [512, 8192], P(None, 'tok'), may hold values from -6 to 6
- query_in: bfloat16 [256, 8192], P(None, 'tok'), may hold values from -6 to 6
- doc_grad: bfloat16 [512, 28672], P('tok', 'feat'), may hold values from -6 to 6
- query_grad: bfloat16 [256, 28672], P('tok', 'feat'), may hold values from -6 to 6
- doc_ids: int32 [512], replicated, may hold values from 0 to 3, as said below
- query_ids: int32 [256], replicated, may hold values from 0 to 1, as said below
- in_basis: bfloat16 [8192, 8192], P('tok', 'feat'), may hold values from -0.0625 to 0.0625
- out_basis: bfloat16 [28672, 28672], P('feat', 'tok'), may hold values from -0.03125 to 0.03125
- eigvals: float32 [8192, 28672], P('feat', 'tok'), may hold values from 0.1 to 10
Outputs:
- ihvp: bfloat16 [8192, 28672], P('feat', 'tok')
- scores: float32 [2, 4], replicated
The draws below stay inside these ranges and needn't reach their ends.
Inputs may be any that keep to these rules, and one draw needn't show every extreme that they name: `doc_ids`: never falling along the tokens; every document has 1 to 256 tokens, one exactly that many. `query_ids`: one transcript has exactly 192 tokens, the other the remaining 256 // 4; their tokens may lie anywhere.
All inputs are finite; a program needn't handle non-finite values.
Results may differ from the reference program's by a relative error of at most 0.012.
Values may be sent and summed in bfloat16 or wider, within the bound.
A program may use at most 128 MiB of HBM per device.

```python
import math
import jax
import jax.numpy as jnp
from jax import lax

D_IN = 8192
D_OUT = 28672
DOCS = 4
QUERIES = 2
DOC_TOK = 512
QUERY_TOK = 256
N_TOK = 64


def draw_doc_ids(key, part):
    key = jax.random.fold_in(key, 11)
    key_big, key_cut = jax.random.split(key)
    half = DOC_TOK // 2
    cuts = jax.random.permutation(key_cut, jnp.arange(1, half, dtype=jnp.int32))[:2]
    cuts = jnp.sort(cuts)
    small = jnp.stack([cuts[0], cuts[1] - cuts[0], half - cuts[1]]).astype(jnp.int32)
    which = jax.random.randint(key_big, (), 0, DOCS, dtype=jnp.int32)
    slots = jnp.arange(DOCS, dtype=jnp.int32)
    picked = jnp.clip(slots - (slots > which).astype(jnp.int32), 0, DOCS - 2)
    lengths = jnp.where(slots == which, half, small[picked]).astype(jnp.int32)
    bounds = jnp.cumsum(lengths)[:DOCS - 1].astype(jnp.int32)
    places = jnp.arange(DOC_TOK, dtype=jnp.int32)
    return jnp.sum((places[:, None] >= bounds[None, :]).astype(jnp.int32), axis=1).astype(jnp.int32)


def draw_query_ids(key, part):
    key = jax.random.fold_in(key, 23)
    key_side, key_perm = jax.random.split(key)
    small_id = jax.random.randint(key_side, (), 0, 2, dtype=jnp.int32)
    order = jax.random.permutation(key_perm, jnp.arange(QUERY_TOK, dtype=jnp.int32))
    in_small = order < QUERY_TOK // 4
    return jnp.where(in_small, small_id, 1 - small_id).astype(jnp.int32)


def level_of(rng, shape, cuts, smallest, top_value):
    level, own = 1.0, jax.random.fold_in(rng, 6)
    for axis_at, parts in cuts:
        steps = jnp.exp(jax.random.uniform(jax.random.fold_in(own, axis_at), (parts,), jnp.float32, smallest / len(cuts), top_value / len(cuts)))
        level = level * jnp.repeat(steps, shape[axis_at] // parts).reshape([-1 if axis == axis_at else 1 for axis in range(len(shape))])
    return level


def centred(key, dims, spread, bound, cuts=(), held_as=jnp.bfloat16):
    entries = spread * jax.random.normal(key, dims, jnp.float32)
    if cuts:
        entries = entries * level_of(key, dims, cuts, -0.22, 0.18)
    return jnp.clip(entries, -bound, bound).astype(held_as)


def setup_inputs(seed: int = 0) -> dict:
    splits = jax.random.split(jax.random.key(seed), 10)
    return {
        "doc_in": centred(splits[0], (DOC_TOK, D_IN), 1.0, 6.0, ((1, 64),)),
        "query_in": centred(splits[1], (QUERY_TOK, D_IN), 1.0, 6.0, ((1, 64),)),
        "doc_grad": centred(splits[2], (DOC_TOK, D_OUT), 1.0, 6.0, ((0, 64), (1, 4))),
        "query_grad": centred(splits[3], (QUERY_TOK, D_OUT), 1.0, 6.0, ((0, 64), (1, 4))),
        "doc_ids": draw_doc_ids(jax.random.fold_in(splits[9], 71), 0),
        "query_ids": draw_query_ids(jax.random.fold_in(splits[9], 71), 0),
        "in_basis": centred(splits[6], (D_IN, D_IN), D_IN ** -0.5, 0.0625, ((0, 64), (1, 4))),
        "out_basis": centred(splits[7], (D_OUT, D_OUT), D_OUT ** -0.5, 0.03125, ((0, 4), (1, 64))),
        "eigvals": jnp.clip(jnp.exp(math.log(10.0) - 4.6051702 * jax.random.uniform(splits[8], (D_IN, D_OUT), jnp.float32) ** level_of(splits[8], (D_IN, D_OUT), ((0, 4), (1, 64)), -0.2, 0.2)), 0.1, 10.0),
    }


damping = 0.1

def reference(doc_in, query_in, doc_grad, query_grad, doc_ids, query_ids, in_basis, out_basis, eigvals):
    doc_in_rot = jnp.dot(doc_in, in_basis, preferred_element_type=jnp.float32).astype(jnp.bfloat16)
    query_in_rot = jnp.dot(query_in, in_basis, preferred_element_type=jnp.float32).astype(jnp.bfloat16)
    doc_hot = (doc_ids[:, None] == jnp.arange(DOCS, dtype=jnp.int32)[None, :]).astype(jnp.float32)
    query_hot = (query_ids[:, None] == jnp.arange(QUERIES, dtype=jnp.int32)[None, :]).astype(jnp.bfloat16)
    width = D_OUT // N_TOK
    scaling = 1.0 / math.sqrt(QUERY_TOK)

    def one_block(block):
        start = (block * width).astype(jnp.int32)
        columns = lax.dynamic_slice_in_dim(out_basis, start, width, 1)
        doc_out_rot = jnp.dot(doc_grad, columns, preferred_element_type=jnp.float32).astype(jnp.bfloat16)
        query_out_rot = jnp.dot(query_grad, columns, preferred_element_type=jnp.float32).astype(jnp.bfloat16)
        damped = (lax.dynamic_slice_in_dim(eigvals, start, width, 1) + damping) * scaling
        precs = []
        for query in range(QUERIES):
            masked = query_in_rot * query_hot[:, query:query + 1]
            grad_q = jnp.dot(masked.T, query_out_rot, preferred_element_type=jnp.float32)
            precs.append((grad_q / damped).astype(jnp.bfloat16))
        total = precs[0].astype(jnp.float32)
        for query in range(1, QUERIES):
            total = total + precs[query].astype(jnp.float32)
        projected = jnp.dot(doc_in_rot, jnp.concatenate(precs, 1), preferred_element_type=jnp.float32)
        doc_out_f = doc_out_rot.astype(jnp.float32)
        token_rows = []
        for query in range(QUERIES):
            token_rows.append(lax.optimization_barrier(jnp.sum(projected[:, query * width:(query + 1) * width] * doc_out_f, axis=1)))
        token_score = jnp.stack(token_rows, 0)
        block_scores = jnp.dot(token_score, doc_hot, precision=lax.Precision.HIGHEST)
        return (total.astype(jnp.bfloat16), block_scores)
    blocks, block_scores = lax.map(one_block, jnp.arange(N_TOK, dtype=jnp.int32))
    ihvp = jnp.transpose(blocks, (1, 0, 2)).reshape(D_IN, D_OUT)
    scores = lax.optimization_barrier(jnp.sum(block_scores, axis=0)) / math.sqrt(D_IN * D_OUT * DOC_TOK)
    return (ihvp, scores)
```

```python
import functools
import math

import jax
import jax.numpy as jnp
from jax import lax
from jax.experimental import pallas as pl
from jax.experimental.pallas import tpu as pltpu
from jax.sharding import PartitionSpec as P

DOCS = 4
QUERIES = 2
DAMPING = 0.1
Y = 4
CORES = 2
RS_DT = jnp.float32
X_DT = jnp.float32
F32 = jnp.float32
BF16 = jnp.bfloat16
MESH = pl.DeviceIdType.MESH
N_SEM = 400


def ds(i, size):
    return pl.ds(pl.multiple_of(i * size, size), size)


def kernel(
    Z, X, scale,
    doc_in, query_in, doc_grad, query_grad, doc_ids, query_ids, in_basis, out_basis, eigvals,
    ihvp, scores,
    inq, ind, inb, gd_own, gd_oth, gq_own, gq_oth, gq_f, gd, gq, gq2, bown, both, eig,
    pin_q, pin_d, zs_q, zr_q, zs_d, zr_d, zsum_q, zsum_d, ys_q, yr_q, ys_d, yr_d, rot_q, rot_d,
    p_own, p_oth, p_rcv, x_snd, x_rcv, out_rot, mq, prec, ih, proj, sc_a, sc_b, sc_c,
    ssem, rsem, lsem,
):
    tok, x = lax.axis_index("tok"), lax.axis_index("feat")
    c = lax.rem(tok, CORES)
    y = lax.rem(lax.div(tok, CORES), Y)
    z = lax.div(tok, CORES * Y)
    oc = 1 - c

    def dev(zz, yy, cc, xx):
        return ((zz * Y + yy) * CORES + cc, xx)

    def wrap(v, n):
        return lax.rem(v + 4 * n, n)

    partner = dev(z, y, oc, x)

    def to_z(step):
        return dev(wrap(z + step, Z), y, c, x)

    def to_y(step):
        return dev(z, wrap(y + step, Y), c, x)

    G = CORES * X
    m = c * X + x

    def to_m(step):
        mm = wrap(m + step, G)
        return dev(z, y, lax.div(mm, X), lax.rem(mm, X))

    barrier = pltpu.get_barrier_semaphore()
    friends = [to_m(k) for k in range(1, G)] + [to_y(k) for k in range(1, Y)] + [to_z(k) for k in range(1, Z)]
    for friend in friends:
        pl.semaphore_signal(barrier, inc=1, device_id=friend, device_id_type=MESH)

    locals_ = []

    def local(src, dst):
        copy = pltpu.make_async_copy(src, dst, lsem.at[len(locals_)])
        copy.start()
        locals_.append(copy)
        return copy

    F = doc_grad.shape[1]
    half = F // 2
    quarter = half // 2
    wc = in_basis.shape[1] // CORES
    nf = in_basis.shape[0]

    l_gq = local(query_grad.at[:, ds(c, half)], gq_own)
    l_inq = local(query_in, inq.at[:, ds(c, nf)])
    l_inb = local(in_basis.at[:, ds(c, wc)], inb.at[ds(c, nf), :])
    l_ind = local(doc_in, ind.at[:, ds(c, nf)])
    l_gd = local(doc_grad.at[:, ds(c, half)], gd_own)
    l_b = local(out_basis.at[ds(c, half), :], bown)
    l_eig = local(eigvals, eig)

    pl.semaphore_wait(barrier, len(friends))

    sent = []

    def send(src, dst, to):
        i = len(sent)
        copy = pltpu.make_async_remote_copy(
            src_ref=src, dst_ref=dst, send_sem=ssem.at[i], recv_sem=rsem.at[i], device_id=to, device_id_type=MESH
        )
        copy.start()
        sent.append(copy)
        return copy

    r_gq = send(query_grad.at[:, ds(oc, half)], gq_oth, partner)
    r_inq = send(query_in, inq.at[:, ds(c, nf)], partner)
    r_inb = send(in_basis.at[:, ds(oc, wc)], inb.at[ds(c, nf), :], partner)
    r_ind = send(doc_in, ind.at[:, ds(c, nf)], partner)
    r_gd = send(doc_grad.at[:, ds(oc, half)], gd_oth, partner)
    r_b = send(out_basis.at[ds(oc, half), :], both, partner)

    def ring_ag(p, n, blk, half_of, to, arrived=lambda k: None):
        h = n // 2
        r = send(blk(p), blk(p), to(1))
        l = send(blk(p), blk(p), to(-1))
        for s in range(1, h):
            yield
            k = wrap(p - s, n)
            r.wait_recv()
            if s < h - 1:
                r = send(blk(k), blk(k), to(1))
            else:
                r = send(half_of(k, 0), half_of(k, 0), to(1))
            arrived(k)
            k = wrap(p + s, n)
            l.wait_recv()
            if s < h - 1:
                l = send(blk(k), blk(k), to(-1))
            else:
                l = send(half_of(k, 1), half_of(k, 1), to(-1))
            arrived(k)
        yield
        r.wait_recv()
        l.wait_recv()
        arrived(wrap(p + h, n))

    def ring_rs(p, n, part, snd, rcv, width, to, done):
        h = n // 2
        lo, hi = slice(0, width // 2), slice(width // 2, width)
        r_half, l_half = rcv.at[0, 0, :, lo], rcv.at[1, 0, :, hi]
        snd[0, 0] = part(wrap(p + h, n)).astype(snd.dtype)
        r = send(snd.at[0, 0, :, lo], r_half, to(1))
        l = send(snd.at[0, 0, :, hi], l_half, to(-1))
        for s in range(1, h):
            yield
            own = part(wrap(p + h - s, n))
            r.wait_recv()
            if s == 1:
                snd[0, s, :, lo] = (own[:, lo] + rcv[0, 0, :, lo].astype(F32)).astype(snd.dtype)
                snd[0, s, :, hi] = own[:, hi].astype(snd.dtype)
            else:
                snd[0, s] = (own + rcv[0, s - 1].astype(F32)).astype(snd.dtype)
            r = send(snd.at[0, s], rcv.at[0, s], to(1))
            own = part(wrap(p - h + s, n))
            l.wait_recv()
            if s == 1:
                snd[1, s, :, lo] = own[:, lo].astype(snd.dtype)
                snd[1, s, :, hi] = (own[:, hi] + rcv[1, 0, :, hi].astype(F32)).astype(snd.dtype)
            else:
                snd[1, s] = (own + rcv[1, s - 1].astype(F32)).astype(snd.dtype)
            l = send(snd.at[1, s], rcv.at[1, s], to(-1))
        yield
        own = part(p)
        r.wait_recv()
        l.wait_recv()
        done(own + rcv[0, h - 1].astype(F32) + rcv[1, h - 1].astype(F32))

    def gd_blk(zz, yy):
        return gd.at[ds(zz * Y + yy, 2 * doc_grad.shape[0]), :]

    def gd_half(zz, yy, k):
        return gd.at[ds(zz * Y + yy, 2 * doc_grad.shape[0]), pl.ds(k * (half // 2), half // 2)]

    def gq_blk(zz, yy):
        return gq.at[zz * Y + yy]

    def gq_half(zz, yy, k):
        return gq.at[zz * Y + yy, :, pl.ds(k * (quarter // 2), quarter // 2)]

    y_q, y_d = [], []

    def spawn_q(zz):
        y_q.append(ring_ag(y, Y, lambda k: gq_blk(zz, k), lambda k, b: gq_half(zz, k, b), to_y))

    def spawn_d(zz):
        y_d.append(ring_ag(y, Y, lambda k: gd_blk(zz, k), lambda k, b: gd_half(zz, k, b), to_y))

    live = []

    def y_step(window=4):
        while len(live) < window and (y_q or y_d):
            task = (y_q or y_d).pop(0)
            next(task)
            live.append(task)
        if not live:
            return False
        task = live.pop(0)
        if next(task, "end") != "end":
            live.append(task)
        return True

    nq = query_grad.shape[0]
    first = c == 0
    l_gq.wait()
    r_gq.wait_recv()
    own, oth = gq_own[...].astype(F32), gq_oth[...].astype(F32)
    gq_f[0:nq, :] = jnp.where(first, own, oth)
    gq_f[nq : 2 * nq, :] = jnp.where(first, oth, own)
    me_zy = z * Y + y
    gq[me_zy] = jnp.concatenate([gq_f[:, 0:quarter], gq_f[:, quarter:half]], axis=0).astype(BF16)
    ag_q = ring_ag(z, Z, lambda k: gq_blk(k, y), lambda k, b: gq_half(k, y, b), to_z, spawn_q)
    next(ag_q)
    spawn_q(z)
    y_step_start = y_q.pop(0)
    next(y_step_start)
    live.append(y_step_start)

    dq, dd = query_in.shape[0], doc_in.shape[0]
    bq, bd = dq // Z, dd // Z
    wy = wc // Y
    for copy in (l_inq, l_inb):
        copy.wait()
    for copy in (r_inq, r_inb):
        copy.wait_recv()
    pin_q[...] = jnp.dot(inq[...], inb[...], preferred_element_type=F32)

    def put_zq(v):
        zsum_q[...] = v

    def put_zd(v):
        zsum_d[...] = v

    rs_q = ring_rs(z, Z, lambda k: pin_q[ds(k, bq), :], zs_q, zr_q, wc, to_z, put_zq)
    next(rs_q)
    l_ind.wait()
    r_ind.wait_recv()

    pin_d[...] = jnp.dot(ind[...], inb[...], preferred_element_type=F32)
    rs_d = ring_rs(z, Z, lambda k: pin_d[ds(k, bd), :], zs_d, zr_d, wc, to_z, put_zd)
    next(rs_d)

    l_gd.wait()
    r_gd.wait_recv()
    own, oth = gd_own[...].astype(F32), gd_oth[...].astype(F32)
    gd[ds(me_zy, 2 * doc_grad.shape[0]), :] = jnp.concatenate(
        [jnp.where(first, own, oth), jnp.where(first, oth, own)], axis=0
    ).astype(BF16)
    ag_d = ring_ag(z, Z, lambda k: gd_blk(k, y), lambda k, b: gd_half(k, y, b), to_z, spawn_d)
    next(ag_d)
    spawn_d(z)

    for _ in range(Z // 2):
        next(rs_q, None)
        next(rs_d, None)
        next(ag_q, None)
        next(ag_d, None)
        for _ in range(4):
            y_step()

    def rows_of(rot, b, k, col, width):
        return rot.at[ds(k, b), ds(col, width)]

    def in_task(rot, zsum, ys, yr, b):
        def part(k):
            return zsum[:, ds(k, wy)]

        def put(v):
            rot[ds(z, b), ds(c * Y + y, wy)] = v.astype(BF16)

        yield from ring_rs(y, Y, part, ys, yr, wy, to_y, put)
        yield from ring_ag(
            y, Y, lambda k: rows_of(rot, b, z, c * Y + k, wy),
            lambda k, h: rows_of(rot, b, z, (c * Y + k) * 2 + h, wy // 2), to_y,
        )
        yield from ring_ag(
            z, Z, lambda k: rows_of(rot, b, k, c, wc),
            lambda k, h: rows_of(rot, b, k, c * 2 + h, wc // 2), to_z,
        )
        whole = rot.at[:, ds(c, wc)]
        copy = send(whole, whole, partner)
        yield
        copy.wait_recv()

    in_q = in_task(rot_q, zsum_q, ys_q, yr_q, bq)
    in_d = in_task(rot_d, zsum_d, ys_d, yr_d, bd)
    next(in_q)
    next(in_d)

    def matmul(lhs, b, out, row, rows, tile=896):
        depth = lhs.shape[1]
        tile = math.gcd(depth, tile)
        out[row : row + rows, :] = jnp.dot(
            lhs[:, 0:tile], b[0:tile, :], preferred_element_type=F32
        )

        def body(k, _):
            out[row : row + rows, :] += jnp.dot(lhs[:, ds(k, tile)], b[ds(k, tile), :], preferred_element_type=F32)
            return 0

        lax.fori_loop(1, depth // tile, body, 0)

    def out_task(lhs, row, rows):
        span = slice(row, row + rows)
        share = rows // X
        base = row // X
        matmul(lhs, both, p_oth, row, rows)
        swap = send(p_oth.at[span, :], p_rcv.at[span, :], partner)
        matmul(lhs, bown, p_own, row, rows)
        yield
        swap.wait_recv()
        total = p_own[span, :] + p_rcv[span, :]
        p_own[span, :] = total
        x_snd[span, :] = total.astype(X_DT)
        copies = []
        for k in range(1, X):
            to = wrap(x + k, X)
            copies.append(
                send(
                    x_snd.at[pl.ds(pl.multiple_of(row + to * share, share), share), :],
                    x_rcv.at[x, pl.ds(base, share), :],
                    dev(z, y, c, to),
                )
            )
        yield
        for copy in copies:
            copy.wait_recv()
        mine = pl.ds(pl.multiple_of(row + x * share, share), share)
        x_rcv[x, pl.ds(base, share), :] = x_snd[mine, :]
        total = x_rcv[0, pl.ds(base, share), :].astype(F32)
        for k in range(1, X):
            total = total + x_rcv[k, pl.ds(base, share), :].astype(F32)
        out_rot[mine, :] = total.astype(BF16)
        copies = []
        for k in range(1, X):
            copies.append(send(out_rot.at[mine, :], out_rot.at[mine, :], dev(z, y, c, wrap(x + k, X))))
        yield
        for copy in copies:
            copy.wait_recv()

    for _ in range(5 + Z // 2 - 2):
        next(in_q, None)
        next(in_d, None)
        for _ in range(2):
            y_step()

    while y_step():
        pass
    l_b.wait()
    r_b.wait_recv()

    for h in range(2):
        rows = gq.shape[1] // 2
        gq2[:, h * quarter : (h + 1) * quarter] = (
            gq[:, h * rows : (h + 1) * rows, :].astype(F32).reshape(dq, quarter).astype(BF16)
        )
    out_q = out_task(gq2, 0, dq)
    next(out_q)
    next(in_q, None)
    next(in_d, None)
    next(out_q)
    out_d = out_task(gd, dq, dd)
    next(out_d)
    next(out_q)
    next(out_d)
    next(out_q, None)

    ids_q = jnp.broadcast_to(query_ids[...].astype(F32), (128, dq)).T[:, 0:1]
    for q in range(QUERIES):
        mq[q] = jnp.where(ids_q == float(q), out_rot[0:dq, :].astype(F32), 0.0).astype(BF16)
    l_eig.wait()
    for _ in range(2):
        next(in_q, None)

    tile = 256
    n_tiles = eig.shape[0] // tile

    def ih_copy(i):
        return pltpu.make_async_copy(ih.at[ds(i, tile), :], ihvp.at[ds(i, tile), :], lsem.at[16 + i])

    def precondition(i, _):
        at = ds(i, tile)
        factor = math.sqrt(dq) / (eig[at, :] + DAMPING)
        lhs = rot_q[:, at]
        total = None
        for q in range(QUERIES):
            grad = lax.dot_general(lhs, mq[q], (((0,), (0,)), ((), ())), preferred_element_type=F32)
            block = (grad * factor).astype(BF16)
            prec[q, at, :] = block
            block = block.astype(F32)
            total = block if total is None else total + block
        ih[at, :] = total.astype(BF16)
        ih_copy(i).start()
        return 0

    lax.fori_loop(0, n_tiles, precondition, 0)
    next(out_d)
    for _ in range(2):
        next(in_d, None)

    for q in range(QUERIES):
        matmul(rot_d, prec.at[q], proj.at[q], 0, dd, 512)
    next(out_d, None)

    ids_d = jnp.broadcast_to(doc_ids[...].astype(F32), (128, dd)).T
    lane = lax.broadcasted_iota(jnp.int32, (dd, 128), 1).astype(F32)
    hot = (ids_d == lane).astype(F32)
    row_id = lax.broadcasted_iota(jnp.int32, (8, 128), 0)
    value = jnp.zeros((8, 128), F32)
    for q in range(QUERIES):
        token = jnp.sum(proj[q] * out_rot[dq : dq + dd, :].astype(F32), axis=1, keepdims=True)
        per_doc = jnp.sum(token * hot, axis=0, keepdims=True)
        value = jnp.where(row_id == q, per_doc, value)

    def exchange(buf, me, n, to, value):
        buf[me] = value
        copies = [send(buf.at[me], buf.at[me], to(k)) for k in range(1, n)]
        for copy in copies:
            copy.wait_recv()
        return jnp.sum(buf[...], axis=0)

    value = exchange(sc_a, m, G, to_m, value)
    value = exchange(sc_b, y, Y, to_y, value)
    value = exchange(sc_c, z, Z, to_z, value)
    scores[...] = value[0:QUERIES, 0:DOCS] * scale

    def ih_wait(i, _):
        ih_copy(i).wait()
        return 0

    lax.fori_loop(0, n_tiles, ih_wait, 0)
    for copy in sent:
        copy.wait_send()


def shards(
    Z, X, doc_in, query_in, doc_grad, query_grad, doc_ids, query_ids, in_basis, out_basis, eigvals
):
    dd, dq = doc_in.shape[0], query_in.shape[0]
    F, cols = out_basis.shape
    half, quarter = F // 2, F // 4
    nf, width = in_basis.shape
    wc = width // CORES
    wy = wc // Y
    bq, bd = dq // Z, dd // Z
    hz, hy = Z // 2, Y // 2
    n_docs, n_q = doc_grad.shape[0], query_grad.shape[0]
    scale = 1.0 / math.sqrt(width * X * cols * Z * Y * CORES * dd)
    vmem = pltpu.VMEM
    any_ = pl.BlockSpec(memory_space=pl.ANY)
    in_vmem = pl.BlockSpec(memory_space=pltpu.VMEM)
    return pl.pallas_call(
        functools.partial(kernel, Z, X, scale),
        out_shape=(
            jax.ShapeDtypeStruct((width, cols), BF16),
            jax.ShapeDtypeStruct((QUERIES, DOCS), F32),
        ),
        in_specs=[any_, any_, any_, any_, in_vmem, in_vmem, any_, any_, any_],
        out_specs=(any_, in_vmem),
        scratch_shapes=[
            vmem((dq, CORES * nf), BF16), vmem((dd, CORES * nf), BF16), vmem((CORES * nf, wc), BF16),
            vmem((n_docs, half), BF16), vmem((n_docs, half), BF16),
            vmem((n_q, half), BF16), vmem((n_q, half), BF16), vmem((2 * n_q, half), F32),
            vmem((dd, half), BF16), vmem((Z * Y, 4 * n_q, quarter), BF16), vmem((dq, half), BF16),
            vmem((half, cols), BF16), vmem((half, cols), BF16), vmem((width, cols), F32),
            vmem((dq, wc), F32), vmem((dd, wc), F32),
            vmem((2, hz, bq, wc), RS_DT), vmem((2, hz, bq, wc), RS_DT),
            vmem((2, hz, bd, wc), RS_DT), vmem((2, hz, bd, wc), RS_DT),
            vmem((bq, wc), F32), vmem((bd, wc), F32),
            vmem((2, hy, bq, wy), F32), vmem((2, hy, bq, wy), F32),
            vmem((2, hy, bd, wy), F32), vmem((2, hy, bd, wy), F32),
            vmem((dq, width), BF16), vmem((dd, width), BF16),
            vmem((dq + dd, cols), F32), vmem((dq + dd, cols), F32), vmem((dq + dd, cols), F32),
            vmem((dq + dd, cols), X_DT), vmem((X, (dq + dd) // X, cols), X_DT), vmem((dq + dd, cols), BF16),
            vmem((QUERIES, dq, cols), BF16), vmem((QUERIES, width, cols), BF16), vmem((width, cols), BF16),
            vmem((QUERIES, dd, cols), F32),
            vmem((CORES * X, 8, 128), F32), vmem((Y, 8, 128), F32), vmem((Z, 8, 128), F32),
            pltpu.SemaphoreType.DMA((N_SEM,)), pltpu.SemaphoreType.DMA((N_SEM,)), pltpu.SemaphoreType.DMA((32,)),
        ],
        compiler_params=pltpu.CompilerParams(
            collective_id=0, has_side_effects=True, vmem_limit_bytes=62 * 1024 * 1024
        ),
    )(
        doc_in, query_in, doc_grad, query_grad, doc_ids.reshape(1, dd), query_ids.reshape(1, dq),
        in_basis, out_basis, eigvals,
    )


def solution(mesh):
    placed = (
        P(None, "tok"),
        P(None, "tok"),
        P("tok", "feat"),
        P("tok", "feat"),
        P(),
        P(),
        P("tok", "feat"),
        P("feat", "tok"),
        P("feat", "tok"),
    )
    X = mesh.shape["feat"]
    Z = mesh.shape["tok"] // (Y * CORES)
    return jax.shard_map(
        functools.partial(shards, Z, X), mesh=mesh, in_specs=placed, out_specs=(P("feat", "tok"), P()), check_vma=False
    )
```

```python
import functools
import math

import jax
import jax.numpy as jnp
from jax import lax
from jax.experimental import pallas as pl
from jax.experimental.pallas import tpu as pltpu
from jax.sharding import PartitionSpec as P

DOCS = 4
QUERIES = 2
DAMPING = 0.1
Y = 4
CORES = 2
RS_DT = jnp.bfloat16
X_DT = jnp.float32
F32 = jnp.float32
BF16 = jnp.bfloat16
MESH = pl.DeviceIdType.MESH
N_SEM = 256
PLAN = (
    "yd0", "q", "yq1", "yq7", "Q", "yq0", "q", "yq2", "D", "Q", "q", "yd0", "yq1", "yq7", "yq0", "yq6", "yq2", "Q",
    "q", "yd0", "yq3", "yq1", "yq5", "D", "yq7", "yq4", "Q", "d", "yq6", "yq2", "yq3", "yq5", "yq4", "Q", "D",
    "yq6", "yq3", "d", "yd1", "yd7", "yq5", "Q", "yq4", "oq", "yd1", "D", "Q", "yd7", "d", "yd2", "yd6", "oq",
    "yd1", "o0", "Q", "D", "yd7", "Q", "o0", "d", "yd3", "yd5", "yd2", "Q", "oq", "Q", "yd6", "d", "yd4", "D", "o0",
    "yd3", "oq", "P", "yd5", "yd2", "o0", "D", "yd6", "o3", "yd4", "yd3", "o1", "o3", "yd5", "D", "yd4", "o2", "o1",
    "o2", "o3", "D", "o1", "D", "o2", "o3", "D", "R", "o1", "o2",
)


def ds(i, size):
    return pl.ds(pl.multiple_of(i * size, size), size)


def kernel(
    Z, X, scale,
    doc_in, query_in, doc_grad, query_grad, doc_ids, query_ids, in_basis, out_basis, eigvals,
    ihvp, scores,
    inq, ind, inb, gd_own, gd_oth, gq_own, gq_oth, gq_f, gd, gq, gq2, bb, eig,
    pin_q, pin_d, zs_q, zr_q, zs_d, zr_d, yr_q, yr_d, rot_q, rot_d,
    part, p_rcv, x_snd, x_rcv, out_rot, mq, prec, ih, proj, sc_a, sc_b, sc_c,
    ssem, rsem, lsem,
):
    tok, x = lax.axis_index("tok"), lax.axis_index("feat")
    c = lax.rem(tok, CORES)
    y = lax.rem(lax.div(tok, CORES), Y)
    z = lax.div(tok, CORES * Y)
    oc = 1 - c

    def dev(zz, yy, cc, xx):
        return ((zz * Y + yy) * CORES + cc, xx)

    def wrap(v, n):
        return lax.rem(v + 4 * n, n)

    partner = dev(z, y, oc, x)

    def to_z(step):
        return dev(wrap(z + step, Z), y, c, x)

    def to_y(step):
        return dev(z, wrap(y + step, Y), c, x)

    G = CORES * X
    m = c * X + x

    def to_m(step):
        mm = wrap(m + step, G)
        return dev(z, y, lax.div(mm, X), lax.rem(mm, X))

    barrier = pltpu.get_barrier_semaphore()
    friends = [to_m(k) for k in range(1, G)] + [to_y(k) for k in range(1, Y)] + [to_z(k) for k in range(1, Z)]
    for friend in friends:
        pl.semaphore_signal(barrier, inc=1, device_id=friend, device_id_type=MESH)

    locals_ = []

    def local(src, dst):
        copy = pltpu.make_async_copy(src, dst, lsem.at[len(locals_)])
        copy.start()
        locals_.append(copy)
        return copy

    F = doc_grad.shape[1]
    half = F // 2
    quarter = half // 2
    wc = in_basis.shape[1] // CORES
    nf = in_basis.shape[0]

    l_gq = local(query_grad.at[:, ds(c, half)], gq_own)
    l_inq = local(query_in, inq.at[:, ds(c, nf)])
    l_inb = local(in_basis.at[:, ds(c, wc)], inb.at[ds(c, nf), :])
    l_ind = local(doc_in, ind.at[:, ds(c, nf)])
    l_gd = local(doc_grad.at[:, ds(c, half)], gd_own)
    cols = out_basis.shape[0]
    theirs, ours = bb.at[0:cols, :], bb.at[cols : 2 * cols, :]
    l_b = local(out_basis.at[:, ds(c, half)], ours)
    l_eig = local(eigvals, eig)

    pl.semaphore_wait(barrier, len(friends))

    sent = []

    def send(src, dst, to):
        i = len(sent)
        copy = pltpu.make_async_remote_copy(
            src_ref=src, dst_ref=dst, send_sem=ssem.at[i], recv_sem=rsem.at[i], device_id=to, device_id_type=MESH
        )
        copy.start()
        sent.append(copy)
        return copy

    r_gq = send(query_grad.at[:, ds(oc, half)], gq_oth, partner)
    r_inq = send(query_in, inq.at[:, ds(c, nf)], partner)
    r_inb = send(in_basis.at[:, ds(oc, wc)], inb.at[ds(c, nf), :], partner)
    r_ind = send(doc_in, ind.at[:, ds(c, nf)], partner)
    r_gd = send(doc_grad.at[:, ds(oc, half)], gd_oth, partner)
    r_b = send(out_basis.at[:, ds(oc, half)], theirs, partner)

    def ring_ag(n, blk, there, to):
        h = n // 2

        def forward(o, step, b):
            return send(blk(o, b), there(o, step, b), to(step))

        r, l = forward(0, 1, None), forward(0, -1, None)
        for s in range(1, h):
            yield
            r.wait_recv()
            r = forward(-s, 1, None if s < h - 1 else 0)
            l.wait_recv()
            l = forward(s, -1, None if s < h - 1 else 1)
        yield
        r.wait_recv()
        l.wait_recv()

    def ring_rs(p, n, own_part, snd, rcv, width, to, done):
        h = n // 2
        lo, hi = slice(0, width // 2), slice(width // 2, width)
        r_half, l_half = rcv.at[0, 0, :, lo], rcv.at[1, 0, :, hi]
        snd[0, 0] = own_part(wrap(p + h, n)).astype(snd.dtype)
        r = send(snd.at[0, 0, :, lo], r_half, to(1))
        l = send(snd.at[0, 0, :, hi], l_half, to(-1))
        for s in range(1, h):
            yield
            own = own_part(wrap(p + h - s, n))
            r.wait_recv()
            if s == 1:
                snd[0, s, :, lo] = (own[:, lo] + rcv[0, 0, :, lo].astype(F32)).astype(snd.dtype)
                snd[0, s, :, hi] = own[:, hi].astype(snd.dtype)
            else:
                snd[0, s] = (own + rcv[0, s - 1].astype(F32)).astype(snd.dtype)
            r = send(snd.at[0, s], rcv.at[0, s], to(1))
            own = own_part(wrap(p - h + s, n))
            l.wait_recv()
            if s == 1:
                snd[1, s, :, lo] = own[:, lo].astype(snd.dtype)
                snd[1, s, :, hi] = (own[:, hi] + rcv[1, 0, :, hi].astype(F32)).astype(snd.dtype)
            else:
                snd[1, s] = (own + rcv[1, s - 1].astype(F32)).astype(snd.dtype)
            l = send(snd.at[1, s], rcv.at[1, s], to(-1))
        yield
        own = own_part(p)
        r.wait_recv()
        l.wait_recv()
        done(own + rcv[0, h - 1].astype(F32) + rcv[1, h - 1].astype(F32))

    rows_d = 2 * doc_grad.shape[0]

    def gd_blk(oz, yy, b=None):
        at = pl.ds(pl.multiple_of((oz % Z) * Y * rows_d + yy * rows_d, rows_d), rows_d)
        return gd.at[at, :] if b is None else gd.at[at, pl.ds(b * quarter, quarter)]

    def gq_blk(oz, yy, b=None):
        at = wrap(z + oz, Z) * Y + yy
        return gq.at[at] if b is None else gq.at[at, :, pl.ds(b * (quarter // 2), quarter // 2)]

    def along_y(blk, oz):
        def place(o, b):
            return blk(oz, wrap(y + o, Y), b)

        return ring_ag(Y, place, lambda o, step, b: place(o, b), to_y)

    tasks = {}
    for oz in range(Z):
        tasks["yq%d" % oz] = along_y(gq_blk, oz)
        tasks["yd%d" % oz] = along_y(gd_blk, oz)

    nq = query_grad.shape[0]
    first = c == 0
    l_gq.wait()
    r_gq.wait_recv()
    own, oth = gq_own[...].astype(F32), gq_oth[...].astype(F32)
    gq_f[0:nq, :] = jnp.where(first, own, oth)
    gq_f[nq : 2 * nq, :] = jnp.where(first, oth, own)
    gq[z * Y + y] = jnp.concatenate([gq_f[:, 0:quarter], gq_f[:, quarter:half]], axis=0).astype(BF16)
    ag_q = ring_ag(Z, lambda o, b: gq_blk(o, y, b), lambda o, step, b: gq_blk(o, y, b), to_z)
    tasks["q"] = ag_q
    next(ag_q)
    next(tasks["yq0"])

    dq, dd = query_in.shape[0], doc_in.shape[0]
    bq, bd = dq // Z, dd // Z
    wy = wc // Y
    for copy in (l_inq, l_inb):
        copy.wait()
    for copy in (r_inq, r_inb):
        copy.wait_recv()
    pin_q[...] = jnp.dot(inq[...], inb[...], preferred_element_type=F32)

    def in_task(pin, zs, zr, yr, rot, rows, place):
        def put(v):
            for k in range(Y):
                yr[Y + k] = v[:, k * wy : (k + 1) * wy]

        yield from ring_rs(z, Z, lambda k: pin[ds(k, rows), :], zs, zr, wc, to_z, put)
        copies = [send(yr.at[Y + wrap(y + k, Y)], yr.at[y], to_y(k)) for k in range(1, Y)]
        yr[y] = yr[Y + y]
        yield
        for copy in copies:
            copy.wait_recv()
        total = yr[0]
        for k in range(1, Y):
            total = total + yr[k]
        mine = rot.at[place(0), ds(c * Y + y, wy)]
        mine[...] = total.astype(BF16)
        copies = [send(mine, mine, to_y(k)) for k in range(1, Y)]
        yield
        for copy in copies:
            copy.wait_recv()

        def at(o, b):
            return rot.at[place(o), ds(c, wc) if b is None else ds(c * 2 + b, wc // 2)]

        def there(o, step, b):
            return rot.at[place(o, step), ds(c, wc) if b is None else ds(c * 2 + b, wc // 2)]

        yield from ring_ag(Z, at, there, to_z)
        whole = rot.at[:, ds(c, wc)]
        copy = send(whole, whole, partner)
        yield
        copy.wait_recv()

    in_q = in_task(pin_q, zs_q, zr_q, yr_q, rot_q, bq, lambda o, step=0: ds(wrap(z + o, Z), bq))
    in_d = in_task(
        pin_d, zs_d, zr_d, yr_d, rot_d, bd, lambda o, step=0: pl.ds(((o - step) % Z) * bd, bd)
    )
    next(in_q)
    l_ind.wait()
    r_ind.wait_recv()
    pin_d[...] = jnp.dot(ind[...], inb[...], preferred_element_type=F32)
    next(in_d)

    l_gd.wait()
    r_gd.wait_recv()
    own, oth = gd_own[...].astype(F32), gd_oth[...].astype(F32)
    gd[ds(y, rows_d), :] = jnp.concatenate(
        [jnp.where(first, own, oth), jnp.where(first, oth, own)], axis=0
    ).astype(BF16)
    ag_d = ring_ag(Z, lambda o, b: gd_blk(o, y, b), lambda o, step, b: gd_blk(o - step, y, b), to_z)
    tasks.update(d=ag_d, Q=in_q, D=in_d)

    def matmul(a, b, out, at, tile):
        depth = a.shape[1]
        tile = math.gcd(depth, tile)
        contract = (((1,), (1,)), ((), ()))
        out[:, at] = lax.dot_general(a[:, 0:tile], b[:, 0:tile], contract, preferred_element_type=F32)

        def body(k, _):
            out[:, at] += lax.dot_general(a[:, ds(k, tile)], b[:, ds(k, tile)], contract, preferred_element_type=F32)
            return 0

        lax.fori_loop(1, depth // tile, body, 0)

    share = cols // X

    def out_task(grads, at):
        matmul(bb, grads, part, at, 896)
        swap = send(part.at[0:cols, at], p_rcv.at[:, at], partner)
        yield
        swap.wait_recv()
        x_snd[:, at] = (part[cols : 2 * cols, at] + p_rcv[:, at]).astype(X_DT)
        copies = []
        for k in range(1, X):
            to = wrap(x + k, X)
            copies.append(send(x_snd.at[ds(to, share), at], x_rcv.at[x, :, at], dev(z, y, c, to)))
        yield
        for copy in copies:
            copy.wait_recv()
        mine = ds(x, share)
        x_rcv[x, :, at] = x_snd[mine, at]
        total = x_rcv[0, :, at].astype(F32)
        for k in range(1, X):
            total = total + x_rcv[k, :, at].astype(F32)
        out_rot[mine, at] = total.astype(BF16)
        copies = []
        for k in range(1, X):
            copies.append(send(out_rot.at[mine, at], out_rot.at[mine, at], dev(z, y, c, wrap(x + k, X))))
        yield
        for copy in copies:
            copy.wait_recv()

    def out_queries():
        l_b.wait()
        r_b.wait_recv()
        rows = gq.shape[1] // 2
        for h in range(2):
            gq2[:, h * quarter : (h + 1) * quarter] = (
                gq[:, h * rows : (h + 1) * rows, :].astype(F32).reshape(dq, quarter).astype(BF16)
            )
        yield from out_task(gq2, slice(0, dq))

    chunk = 2 * (dd // Z)
    tasks["oq"] = out_queries()
    for i in range(Z // 2):
        tasks["o%d" % i] = out_task(
            gd.at[i * chunk : (i + 1) * chunk, :], slice(dq + i * chunk, dq + (i + 1) * chunk)
        )

    tile = 256
    n_tiles = eig.shape[1] // tile

    def ih_copy(i):
        return pltpu.make_async_copy(ih.at[:, ds(i, tile)], ihvp.at[:, ds(i, tile)], lsem.at[16 + i])

    def precondition(i, _):
        at = ds(i, tile)
        factor = math.sqrt(dq) / (eig[:, at] + DAMPING)
        grad = jnp.dot(mq[...], rot_q[:, at], preferred_element_type=F32)
        total = None
        for q in range(QUERIES):
            block = (grad[q * cols : (q + 1) * cols] * factor).astype(BF16)
            prec[q * cols : (q + 1) * cols, at] = block
            block = block.astype(F32)
            total = block if total is None else total + block
        ih[:, at] = total.astype(BF16)
        ih_copy(i).start()
        return 0

    def precondition_all():
        ids_q = query_ids[...]
        for q in range(QUERIES):
            mq[q * cols : (q + 1) * cols, :] = jnp.where(ids_q == q, out_rot[:, 0:dq].astype(F32), 0.0).astype(BF16)
        l_eig.wait()
        lax.fori_loop(0, n_tiles, precondition, 0)
        yield

    def project():
        matmul(prec, rot_d, proj, slice(0, dd), 512)
        yield

    tasks.update(P=precondition_all(), R=project())
    for name in PLAN:
        next(tasks[name], None)
    for task in tasks.values():
        for _ in task:
            pass

    ids_d = pltpu.roll(jnp.broadcast_to(doc_ids[...], (8, dd)), dd - z * (dd // Z), 1)
    hot = ids_d == lax.broadcasted_iota(jnp.int32, (8, dd), 0)
    row_id = lax.broadcasted_iota(jnp.int32, (8, 128), 0)
    lane_id = lax.broadcasted_iota(jnp.int32, (8, 128), 1)
    value = jnp.zeros((8, 128), F32)
    for q in range(QUERIES):
        token = jnp.sum(
            proj[q * cols : (q + 1) * cols, :] * out_rot[:, dq : dq + dd].astype(F32), axis=0, keepdims=True
        )
        per_doc = jnp.sum(jnp.where(hot, token, 0.0), axis=1, keepdims=True)
        for d in range(DOCS):
            value = jnp.where((row_id == q) & (lane_id == d), per_doc[d : d + 1, :], value)

    def exchange(buf, me, n, to, value):
        buf[me] = value
        copies = [send(buf.at[me], buf.at[me], to(k)) for k in range(1, n)]
        for copy in copies:
            copy.wait_recv()
        return jnp.sum(buf[...], axis=0)

    value = exchange(sc_a, m, G, to_m, value)
    value = exchange(sc_b, y, Y, to_y, value)
    value = exchange(sc_c, z, Z, to_z, value)
    scores[...] = value[0:QUERIES, 0:DOCS] * scale

    def ih_wait(i, _):
        ih_copy(i).wait()
        return 0

    lax.fori_loop(0, n_tiles, ih_wait, 0)
    for copy in sent:
        copy.wait_send()


def shards(
    Z, X, doc_in, query_in, doc_grad, query_grad, doc_ids, query_ids, in_basis, out_basis, eigvals
):
    dd, dq = doc_in.shape[0], query_in.shape[0]
    out_basis = out_basis.T
    cols, F = out_basis.shape
    half, quarter = F // 2, F // 4
    nf, width = in_basis.shape
    wc = width // CORES
    wy = wc // Y
    bq, bd = dq // Z, dd // Z
    hz = Z // 2
    n_docs, n_q = doc_grad.shape[0], query_grad.shape[0]
    scale = 1.0 / math.sqrt(width * X * cols * Z * Y * CORES * dd)
    vmem = pltpu.VMEM
    any_ = pl.BlockSpec(memory_space=pl.ANY)
    in_vmem = pl.BlockSpec(memory_space=pltpu.VMEM)
    ihvp, scores = pl.pallas_call(
        functools.partial(kernel, Z, X, scale),
        out_shape=(
            jax.ShapeDtypeStruct((cols, width), BF16),
            jax.ShapeDtypeStruct((QUERIES, DOCS), F32),
        ),
        in_specs=[any_, any_, any_, any_, in_vmem, in_vmem, any_, any_, any_],
        out_specs=(any_, in_vmem),
        scratch_shapes=[
            vmem((dq, CORES * nf), BF16), vmem((dd, CORES * nf), BF16), vmem((CORES * nf, wc), BF16),
            vmem((n_docs, half), BF16), vmem((n_docs, half), BF16),
            vmem((n_q, half), BF16), vmem((n_q, half), BF16), vmem((2 * n_q, half), F32),
            vmem((dd, half), BF16), vmem((Z * Y, 4 * n_q, quarter), BF16), vmem((dq, half), BF16),
            vmem((2 * cols, half), BF16), vmem((cols, width), F32),
            vmem((dq, wc), F32), vmem((dd, wc), F32),
            vmem((2, hz, bq, wc), RS_DT), vmem((2, hz, bq, wc), RS_DT),
            vmem((2, hz, bd, wc), RS_DT), vmem((2, hz, bd, wc), RS_DT),
            vmem((2 * Y, bq, wy), F32), vmem((2 * Y, bd, wy), F32),
            vmem((dq, width), BF16), vmem((dd, width), BF16),
            vmem((2 * cols, dq + dd), F32), vmem((cols, dq + dd), F32),
            vmem((cols, dq + dd), X_DT), vmem((X, cols // X, dq + dd), X_DT), vmem((cols, dq + dd), BF16),
            vmem((QUERIES * cols, dq), BF16), vmem((QUERIES * cols, width), BF16), vmem((cols, width), BF16),
            vmem((QUERIES * cols, dd), F32),
            vmem((CORES * X, 8, 128), F32), vmem((Y, 8, 128), F32), vmem((Z, 8, 128), F32),
            pltpu.SemaphoreType.DMA((N_SEM,)), pltpu.SemaphoreType.DMA((N_SEM,)), pltpu.SemaphoreType.DMA((32,)),
        ],
        compiler_params=pltpu.CompilerParams(
            collective_id=0, has_side_effects=True, vmem_limit_bytes=62 * 1024 * 1024
        ),
    )(
        doc_in, query_in, doc_grad, query_grad, doc_ids.reshape(1, dd), query_ids.reshape(1, dq),
        in_basis, out_basis, eigvals.T,
    )
    return ihvp.T, scores


def solution(mesh):
    placed = (
        P(None, "tok"),
        P(None, "tok"),
        P("tok", "feat"),
        P("tok", "feat"),
        P(),
        P(),
        P("tok", "feat"),
        P("feat", "tok"),
        P("feat", "tok"),
    )
    X = mesh.shape["feat"]
    Z = mesh.shape["tok"] // (Y * CORES)
    return jax.shard_map(
        functools.partial(shards, Z, X), mesh=mesh, in_specs=placed, out_specs=(P("feat", "tok"), P()), check_vma=False
    )
```

```python
import functools
import math

import jax
import jax.numpy as jnp
from jax import lax
from jax.experimental import pallas as pl
from jax.experimental.pallas import tpu as pltpu
from jax.sharding import PartitionSpec as P

DOCS = 4
QUERIES = 2
DAMPING = 0.1
Y = 4
CORES = 2
RS_DT = jnp.bfloat16
X_DT = jnp.float32
F32 = jnp.float32
BF16 = jnp.bfloat16
MESH = pl.DeviceIdType.MESH
N_SEM = 256
SHIFTED = 1024
PLAN = (
    "yd0", "yq0", "q", "yq1", "yq7", "Q", "x", "D", "yd0", "F", "F", "F", "F", "q", "yq0", "yq2", "F", "F", "yq1",
    "Q", "F", "F", "x", "yq7", "F", "D", "yd0", "yq6", "q", "yq2", "x", "yq1", "yq3", "Q", "yq7", "yq5", "yq6", "d",
    "yq2", "D", "q", "yq4", "yq3", "x", "yq5", "yq6", "yq4", "Q", "d", "yd1", "yq3", "yd7", "yq5", "yq4", "oq", "Q",
    "D", "yd1", "x", "oq", "yd7", "d", "yd2", "yd6", "Q", "x", "D", "yd1", "d", "yd7", "yd3", "yd2", "oq", "Q", "x",
    "o0", "d", "yd6", "D", "Q", "o0", "yd5", "oq", "yd3", "yd2", "yd4", "E", "yd6", "o3", "D", "yd5", "o0", "yd3",
    "o1", "o3", "yd4", "E", "Q", "yd5", "D", "o0", "o1", "yd4", "o2", "E", "o3", "Q", "D", "o2", "o1", "E", "Q",
    "P", "P", "P", "P", "P", "o3", "D", "P", "P", "E", "P", "P", "o2", "D", "R", "R", "R", "S", "o1", "S", "S", "o2",
)


def ds(i, size):
    return pl.ds(pl.multiple_of(i * size, size), size)


def kernel(
    Z, X, scale,
    doc_in, query_in, doc_grad, query_grad, doc_ids, query_ids, in_basis, out_basis, eigvals,
    ihvp, scores,
    inq, ind, inb, gd_own, gd_oth, gq_own, gq_oth, gq_f, gd, gq, gq2, bb, eig,
    pin_q, pin_d, zs_q, zr_q, zs_d, zr_d, yr_q, yr_d, rot_q, rot_d,
    part, p_rcv, x_snd, x_rcv, out_rot, mq, prec, ih, proj, sc_a, sc_b, sc_c,
    ssem, rsem, lsem,
):
    tok, x = lax.axis_index("tok"), lax.axis_index("feat")
    c = lax.rem(tok, CORES)
    y = lax.rem(lax.div(tok, CORES), Y)
    z = lax.div(tok, CORES * Y)
    oc = 1 - c

    def dev(zz, yy, cc, xx):
        return ((zz * Y + yy) * CORES + cc, xx)

    def wrap(v, n):
        return lax.rem(v + 4 * n, n)

    partner = dev(z, y, oc, x)

    def to_z(step):
        return dev(wrap(z + step, Z), y, c, x)

    def to_y(step):
        return dev(z, wrap(y + step, Y), c, x)

    G = CORES * X
    m = c * X + x

    def to_m(step):
        mm = wrap(m + step, G)
        return dev(z, y, lax.div(mm, X), lax.rem(mm, X))

    barrier = pltpu.get_barrier_semaphore()
    friends = [to_m(k) for k in range(1, G)] + [to_y(1), to_y(-1), to_z(1), to_z(-1)]
    for friend in friends:
        pl.semaphore_signal(barrier, inc=1, device_id=friend, device_id_type=MESH)

    locals_ = []

    def local(src, dst):
        copy = pltpu.make_async_copy(src, dst, lsem.at[len(locals_)])
        copy.start()
        locals_.append(copy)
        return copy

    F = doc_grad.shape[1]
    half = F // 2
    quarter = half // 2
    wc = in_basis.shape[1] // CORES
    nf = in_basis.shape[0]

    l_gq = local(query_grad.at[:, ds(c, half)], gq_own)
    l_inq = local(query_in, inq.at[:, ds(c, nf)])
    l_inb = local(in_basis.at[:, ds(c, wc)], inb.at[ds(c, nf), :])
    l_ind = local(doc_in, ind.at[:, ds(c, nf)])
    l_gd = local(doc_grad.at[:, ds(c, half)], gd_own)
    cols = out_basis.shape[0]
    theirs, ours = bb.at[0:cols, :], bb.at[cols : 2 * cols, :]
    l_b = local(out_basis.at[:, ds(c, half)], ours)
    l_eig = local(eigvals, eig)

    pl.semaphore_wait(barrier, len(friends))

    sent = []

    def send(src, dst, to):
        i = len(sent)
        copy = pltpu.make_async_remote_copy(
            src_ref=src, dst_ref=dst, send_sem=ssem.at[i], recv_sem=rsem.at[i], device_id=to, device_id_type=MESH
        )
        copy.start()
        sent.append(copy)
        return copy

    r_gq = send(query_grad.at[:, ds(oc, half)], gq_oth, partner)
    r_inq = send(query_in, inq.at[:, ds(c, nf)], partner)
    r_inb = send(in_basis.at[:, ds(oc, wc)], inb.at[ds(c, nf), :], partner)
    r_ind = send(doc_in, ind.at[:, ds(c, nf)], partner)
    r_gd = send(doc_grad.at[:, ds(oc, half)], gd_oth, partner)
    r_b = send(out_basis.at[:, ds(oc, half)], theirs, partner)

    def ring_ag(n, blk, there, to):
        h = n // 2

        def forward(o, step, b):
            return send(blk(o, b), there(o, step, b), to(step))

        r, l = forward(0, 1, None), forward(0, -1, None)
        for s in range(1, h):
            yield
            r.wait_recv()
            r = forward(-s, 1, None if s < h - 1 else 0)
            l.wait_recv()
            l = forward(s, -1, None if s < h - 1 else 1)
        yield
        r.wait_recv()
        l.wait_recv()

    def ring_rs(p, n, own_part, snd, rcv, width, to, done):
        h = n // 2
        lo, hi = slice(0, width // 2), slice(width // 2, width)
        r_half, l_half = rcv.at[0, 0, :, lo], rcv.at[1, 0, :, hi]
        snd[0, 0] = own_part(wrap(p + h, n)).astype(snd.dtype)
        r = send(snd.at[0, 0, :, lo], r_half, to(1))
        l = send(snd.at[0, 0, :, hi], l_half, to(-1))
        for s in range(1, h):
            yield
            own = own_part(wrap(p + h - s, n))
            r.wait_recv()
            if s == 1:
                snd[0, s, :, lo] = (own[:, lo] + rcv[0, 0, :, lo].astype(F32)).astype(snd.dtype)
                snd[0, s, :, hi] = own[:, hi].astype(snd.dtype)
            else:
                snd[0, s] = (own + rcv[0, s - 1].astype(F32)).astype(snd.dtype)
            r = send(snd.at[0, s], rcv.at[0, s], to(1))
            own = own_part(wrap(p - h + s, n))
            l.wait_recv()
            if s == 1:
                snd[1, s, :, lo] = own[:, lo].astype(snd.dtype)
                snd[1, s, :, hi] = (own[:, hi] + rcv[1, 0, :, hi].astype(F32)).astype(snd.dtype)
            else:
                snd[1, s] = (own + rcv[1, s - 1].astype(F32)).astype(snd.dtype)
            l = send(snd.at[1, s], rcv.at[1, s], to(-1))
        yield
        own = own_part(p)
        r.wait_recv()
        l.wait_recv()
        done(own + rcv[0, h - 1].astype(F32) + rcv[1, h - 1].astype(F32))

    rows_d = 2 * doc_grad.shape[0]

    shifted = min(SHIFTED, quarter)
    main = half - shifted

    def span(first, size, b):
        return pl.ds(first, size) if b is None else pl.ds(first + b * (size // 2), size // 2)

    def gd_rows(oz, yy):
        return pl.ds(pl.multiple_of((oz % Z) * Y * rows_d + yy * rows_d, rows_d), rows_d)

    def gd_blk(oz, yy, b=None):
        return gd.at[gd_rows(oz, yy), span(0, main, b)]

    def shift_task():
        def along(o, b):
            return gd.at[gd_rows(0, wrap(y + o, Y)), span(main, shifted, b)]

        def group(oz, b):
            return gd.at[pl.ds((oz % Z) * Y * rows_d, Y * rows_d), span(main, shifted, b)]

        yield from ring_ag(Y, along, lambda o, step, b: along(o, b), to_y)
        yield from ring_ag(Z, group, lambda o, step, b: group(o - step, b), to_z)

    def gq_blk(oz, yy, b=None):
        at = wrap(z + oz, Z) * Y + yy
        return gq.at[at] if b is None else gq.at[at, :, pl.ds(b * (quarter // 2), quarter // 2)]

    def along_y(blk, oz):
        def place(o, b):
            return blk(oz, wrap(y + o, Y), b)

        return ring_ag(Y, place, lambda o, step, b: place(o, b), to_y)

    tasks = {}
    for oz in range(Z):
        tasks["yq%d" % oz] = along_y(gq_blk, oz)
        tasks["yd%d" % oz] = along_y(gd_blk, oz)

    nq = query_grad.shape[0]
    first = c == 0
    l_gq.wait()
    r_gq.wait_recv()
    own, oth = gq_own[...].astype(F32), gq_oth[...].astype(F32)
    gq_f[0:nq, :] = jnp.where(first, own, oth)
    gq_f[nq : 2 * nq, :] = jnp.where(first, oth, own)
    gq[z * Y + y] = jnp.concatenate([gq_f[:, 0:quarter], gq_f[:, quarter:half]], axis=0).astype(BF16)
    ag_q = ring_ag(Z, lambda o, b: gq_blk(o, y, b), lambda o, step, b: gq_blk(o, y, b), to_z)
    tasks["q"] = ag_q
    next(ag_q)
    next(tasks["yq0"])

    dq, dd = query_in.shape[0], doc_in.shape[0]
    bq, bd = dq // Z, dd // Z
    wy = wc // Y
    for copy in (l_inq, l_inb):
        copy.wait()
    for copy in (r_inq, r_inb):
        copy.wait_recv()
    pin_q[...] = jnp.dot(inq[...], inb[...], preferred_element_type=F32)

    def in_task(pin, zs, zr, yr, rot, rows, place, rest):
        def put(v):
            for k in range(Y):
                yr[Y + k] = v[:, k * wy : (k + 1) * wy]

        yield from ring_rs(z, Z, lambda k: pin[ds(k, rows), :], zs, zr, wc, to_z, put)
        copies = [send(yr.at[Y + wrap(y + k, Y)], yr.at[y], to_y(k)) for k in range(1, Y)]
        yr[y] = yr[Y + y]
        yield
        for copy in copies:
            copy.wait_recv()
        total = yr[0]
        for k in range(1, Y):
            total = total + yr[k]
        mine = rot.at[place(0), ds(c * Y + y, wy)]
        mine[...] = total.astype(BF16)
        copies = [send(mine, mine, to_y(k)) for k in range(1, Y)]
        yield
        for copy in copies:
            copy.wait_recv()

        for name in rest:
            next(tasks[name])
        yield from spread(rot, place, 0, len(rest) + 1)

    def spread(rot, place, i, parts):
        size = wc // parts

        def cols_of(b):
            first, width = (c * parts + i, size) if b is None else ((c * parts + i) * 2 + b, size // 2)
            return ds(first, width)

        yield from ring_ag(
            Z, lambda o, b: rot.at[place(o), cols_of(b)], lambda o, step, b: rot.at[place(o, step), cols_of(b)], to_z
        )
        part = rot.at[:, cols_of(None)]
        copy = send(part, part, partner)
        yield
        copy.wait_recv()

    def place_q(o, step=0):
        return ds(wrap(z + o, Z), bq)

    def place_d(o, step=0):
        return pl.ds(((o - step) % Z) * bd, bd)

    in_q = in_task(pin_q, zs_q, zr_q, yr_q, rot_q, bq, place_q, ())
    in_d = in_task(pin_d, zs_d, zr_d, yr_d, rot_d, bd, place_d, ("E",))
    tasks["E"] = spread(rot_d, place_d, 1, 2)
    next(in_q)
    l_ind.wait()
    r_ind.wait_recv()
    pin_d[...] = jnp.dot(ind[...], inb[...], preferred_element_type=F32)
    next(in_d)

    l_gd.wait()
    r_gd.wait_recv()
    own, oth = gd_own[...].astype(F32), gd_oth[...].astype(F32)
    gd[ds(y, rows_d), :] = jnp.concatenate(
        [jnp.where(first, own, oth), jnp.where(first, oth, own)], axis=0
    ).astype(BF16)
    ag_d = ring_ag(Z, lambda o, b: gd_blk(o, y, b), lambda o, step, b: gd_blk(o - step, y, b), to_z)
    tasks.update(d=ag_d, x=shift_task(), Q=in_q, D=in_d)

    def matmul(a, b, out, at, tile):
        depth = a.shape[1]
        tile = math.gcd(depth, tile)
        contract = (((1,), (1,)), ((), ()))
        out[:, at] = lax.dot_general(a[:, 0:tile], b[:, 0:tile], contract, preferred_element_type=F32)

        def body(k, _):
            out[:, at] += lax.dot_general(a[:, ds(k, tile)], b[:, ds(k, tile)], contract, preferred_element_type=F32)
            return 0

        lax.fori_loop(1, depth // tile, body, 0)

    share = cols // X

    def out_task(grads, at):
        matmul(bb, grads, part, at, 896)
        swap = send(part.at[0:cols, at], p_rcv.at[:, at], partner)
        yield
        swap.wait_recv()
        x_snd[:, at] = (part[cols : 2 * cols, at] + p_rcv[:, at]).astype(X_DT)
        copies = []
        for k in range(1, X):
            to = wrap(x + k, X)
            copies.append(send(x_snd.at[ds(to, share), at], x_rcv.at[x, :, at], dev(z, y, c, to)))
        yield
        for copy in copies:
            copy.wait_recv()
        mine = ds(x, share)
        x_rcv[x, :, at] = x_snd[mine, at]
        total = x_rcv[0, :, at].astype(F32)
        for k in range(1, X):
            total = total + x_rcv[k, :, at].astype(F32)
        out_rot[mine, at] = total.astype(BF16)
        copies = []
        for k in range(1, X):
            copies.append(send(out_rot.at[mine, at], out_rot.at[mine, at], dev(z, y, c, wrap(x + k, X))))
        yield
        for copy in copies:
            copy.wait_recv()

    def out_queries():
        l_b.wait()
        r_b.wait_recv()
        rows = gq.shape[1] // 2
        for h in range(2):
            gq2[:, h * quarter : (h + 1) * quarter] = (
                gq[:, h * rows : (h + 1) * rows, :].astype(F32).reshape(dq, quarter).astype(BF16)
            )
        yield from out_task(gq2, slice(0, dq))

    chunk = 2 * (dd // Z)
    tasks["oq"] = out_queries()
    for i in range(Z // 2):
        tasks["o%d" % i] = out_task(
            gd.at[i * chunk : (i + 1) * chunk, :], slice(dq + i * chunk, dq + (i + 1) * chunk)
        )

    tile = 256
    n_tiles = eig.shape[1] // tile

    def ih_copy(i):
        return pltpu.make_async_copy(ih.at[:, ds(i, tile)], ihvp.at[:, ds(i, tile)], lsem.at[16 + i])

    def precondition(i):
        at = ds(i, tile)
        factor = eig[:, at]
        grad = jnp.dot(mq[...], rot_q[:, at], preferred_element_type=F32)
        total = None
        for q in range(QUERIES):
            block = (grad[q * cols : (q + 1) * cols] * factor).astype(BF16)
            prec[q * cols : (q + 1) * cols, at] = block
            block = block.astype(F32)
            total = block if total is None else total + block
        ih[:, at] = total.astype(BF16)
        ih_copy(i).start()

    def factors():
        yield
        l_eig.wait()
        for i in range(n_tiles):
            if i:
                yield
            at = ds(i, tile)
            eig[:, at] = math.sqrt(dq) / (eig[:, at] + DAMPING)

    def precondition_all():
        yield
        ids_q = query_ids[...]
        for q in range(QUERIES):
            mq[q * cols : (q + 1) * cols, :] = jnp.where(ids_q == q, out_rot[:, 0:dq].astype(F32), 0.0).astype(BF16)
        for i in range(n_tiles):
            if i:
                yield
            precondition(i)

    def project(i):
        size = wc // 2
        for core in range(CORES):
            yield
            at = slice(core * wc + i * size, core * wc + (i + 1) * size)
            block = lax.dot_general(
                prec[:, at], rot_d[:, at], (((1,), (1,)), ((), ())), preferred_element_type=F32
            )
            proj[...] = block if i + core == 0 else proj[...] + block

    tasks.update(F=factors(), P=precondition_all(), R=project(0), S=project(1))
    for name in PLAN:
        next(tasks[name], None)
    for task in tasks.values():
        for _ in task:
            pass

    ids_d = pltpu.roll(jnp.broadcast_to(doc_ids[...], (8, dd)), dd - z * (dd // Z), 1)
    hot = ids_d == lax.broadcasted_iota(jnp.int32, (8, dd), 0)
    row_id = lax.broadcasted_iota(jnp.int32, (8, 128), 0)
    lane_id = lax.broadcasted_iota(jnp.int32, (8, 128), 1)
    value = jnp.zeros((8, 128), F32)
    for q in range(QUERIES):
        token = jnp.sum(
            proj[q * cols : (q + 1) * cols, :] * out_rot[:, dq : dq + dd].astype(F32), axis=0, keepdims=True
        )
        per_doc = jnp.sum(jnp.where(hot, token, 0.0), axis=1, keepdims=True)
        for d in range(DOCS):
            value = jnp.where((row_id == q) & (lane_id == d), per_doc[d : d + 1, :], value)

    def exchange(buf, me, n, to, value):
        buf[me] = value
        copies = [send(buf.at[me], buf.at[me], to(k)) for k in range(1, n)]
        for copy in copies:
            copy.wait_recv()
        return jnp.sum(buf[...], axis=0)

    value = exchange(sc_a, m, G, to_m, value)
    value = exchange(sc_b, y, Y, to_y, value)
    value = exchange(sc_c, z, Z, to_z, value)
    scores[...] = value[0:QUERIES, 0:DOCS] * scale

    def ih_wait(i, _):
        ih_copy(i).wait()
        return 0

    lax.fori_loop(0, n_tiles, ih_wait, 0)
    for copy in sent:
        copy.wait_send()


def shards(
    Z, X, doc_in, query_in, doc_grad, query_grad, doc_ids, query_ids, in_basis, out_basis, eigvals
):
    dd, dq = doc_in.shape[0], query_in.shape[0]
    out_basis = out_basis.T
    cols, F = out_basis.shape
    half, quarter = F // 2, F // 4
    nf, width = in_basis.shape
    wc = width // CORES
    wy = wc // Y
    bq, bd = dq // Z, dd // Z
    hz = Z // 2
    n_docs, n_q = doc_grad.shape[0], query_grad.shape[0]
    scale = 1.0 / math.sqrt(width * X * cols * Z * Y * CORES * dd)
    vmem = pltpu.VMEM
    any_ = pl.BlockSpec(memory_space=pl.ANY)
    in_vmem = pl.BlockSpec(memory_space=pltpu.VMEM)
    ihvp, scores = pl.pallas_call(
        functools.partial(kernel, Z, X, scale),
        out_shape=(
            jax.ShapeDtypeStruct((cols, width), BF16),
            jax.ShapeDtypeStruct((QUERIES, DOCS), F32),
        ),
        in_specs=[any_, any_, any_, any_, in_vmem, in_vmem, any_, any_, any_],
        out_specs=(any_, in_vmem),
        scratch_shapes=[
            vmem((dq, CORES * nf), BF16), vmem((dd, CORES * nf), BF16), vmem((CORES * nf, wc), BF16),
            vmem((n_docs, half), BF16), vmem((n_docs, half), BF16),
            vmem((n_q, half), BF16), vmem((n_q, half), BF16), vmem((2 * n_q, half), F32),
            vmem((dd, half), BF16), vmem((Z * Y, 4 * n_q, quarter), BF16), vmem((dq, half), BF16),
            vmem((2 * cols, half), BF16), vmem((cols, width), F32),
            vmem((dq, wc), F32), vmem((dd, wc), F32),
            vmem((2, hz, bq, wc), RS_DT), vmem((2, hz, bq, wc), RS_DT),
            vmem((2, hz, bd, wc), RS_DT), vmem((2, hz, bd, wc), RS_DT),
            vmem((2 * Y, bq, wy), F32), vmem((2 * Y, bd, wy), F32),
            vmem((dq, width), BF16), vmem((dd, width), BF16),
            vmem((2 * cols, dq + dd), F32), vmem((cols, dq + dd), F32),
            vmem((cols, dq + dd), X_DT), vmem((X, cols // X, dq + dd), X_DT), vmem((cols, dq + dd), BF16),
            vmem((QUERIES * cols, dq), BF16), vmem((QUERIES * cols, width), BF16), vmem((cols, width), BF16),
            vmem((QUERIES * cols, dd), F32),
            vmem((CORES * X, 8, 128), F32), vmem((Y, 8, 128), F32), vmem((Z, 8, 128), F32),
            pltpu.SemaphoreType.DMA((N_SEM,)), pltpu.SemaphoreType.DMA((N_SEM,)), pltpu.SemaphoreType.DMA((32,)),
        ],
        compiler_params=pltpu.CompilerParams(
            collective_id=0, has_side_effects=True, vmem_limit_bytes=62 * 1024 * 1024
        ),
    )(
        doc_in, query_in, doc_grad, query_grad, doc_ids.reshape(1, dd), query_ids.reshape(1, dq),
        in_basis, out_basis, eigvals.T,
    )
    return ihvp.T, scores


def solution(mesh):
    placed = (
        P(None, "tok"),
        P(None, "tok"),
        P("tok", "feat"),
        P("tok", "feat"),
        P(),
        P(),
        P("tok", "feat"),
        P("feat", "tok"),
        P("feat", "tok"),
    )
    X = mesh.shape["feat"]
    Z = mesh.shape["tok"] // (Y * CORES)
    return jax.shard_map(
        functools.partial(shards, Z, X), mesh=mesh, in_specs=placed, out_specs=(P("feat", "tok"), P()), check_vma=False
    )
```

```python
import functools
import math

import jax
import jax.numpy as jnp
from jax import lax
from jax.experimental import pallas as pl
from jax.experimental.pallas import tpu as pltpu
from jax.sharding import PartitionSpec as P

DOCS = 4
QUERIES = 2
DAMPING = 0.1
Y = 4
CORES = 2
RS_DT = jnp.bfloat16
X_DT = jnp.float32
F32 = jnp.float32
BF16 = jnp.bfloat16
MESH = pl.DeviceIdType.MESH
N_SEM = 256
SHIFTED = 1024
PLAN = (
    "yd0", "yq0", "q", "yq1", "yq7", "Q", "x", "D", "yd0", "F", "F", "F", "F", "q", "yq0", "yq2", "F", "F", "yq1",
    "Q", "F", "F", "x", "yq7", "F", "D", "yd0", "yq6", "q", "yq2", "x", "yq1", "yq3", "Q", "yq7", "yq5", "yq6", "d",
    "yq2", "D", "q", "yq4", "yq3", "x", "yq5", "yq6", "yq4", "Q", "d", "yd1", "yq3", "yd7", "yq5", "yq4", "oq", "Q",
    "D", "yd1", "x", "oq", "yd7", "d", "yd2", "yd6", "Q", "x", "D", "yd1", "d", "yd7", "yd3", "yd2", "oq", "Q", "x",
    "o0", "d", "yd6", "D", "Q", "o0", "yd5", "oq", "yd3", "yd2", "yd4", "E", "yd6", "o3", "D", "yd5", "o0", "yd3",
    "o1", "o3", "yd4", "E", "Q", "yd5", "D", "o0", "o1", "yd4", "o2", "E", "o3", "Q", "D", "o2", "o1", "E", "Q",
    "P", "P", "P", "P", "P", "o3", "D", "P", "P", "E", "P", "P", "o2", "D", "R", "R", "R", "S", "o1", "S", "S", "o2",
)


def ds(i, size):
    return pl.ds(pl.multiple_of(i * size, size), size)


def kernel(
    Z, X, scale,
    doc_in, query_in, doc_grad, query_grad, doc_ids, query_ids, in_basis, out_basis, eigvals,
    ihvp, scores,
    inq, ind, inb, gd_own, gd_oth, gq_own, gq_oth, gq_f, gd, gq, gq2, bb, eig,
    pin_q, pin_d, zs_q, zr_q, zs_d, zr_d, yr_q, yr_d, rot_q, rot_d,
    part, p_rcv, x_snd, x_rcv, out_rot, mq, prec, proj, sc_a, sc_b, sc_c,
    ssem, rsem, lsem,
):
    tok, x = lax.axis_index("tok"), lax.axis_index("feat")
    c = lax.rem(tok, CORES)
    y = lax.rem(lax.div(tok, CORES), Y)
    z = lax.div(tok, CORES * Y)
    oc = 1 - c

    def dev(zz, yy, cc, xx):
        return ((zz * Y + yy) * CORES + cc, xx)

    def wrap(v, n):
        return lax.rem(v + 4 * n, n)

    partner = dev(z, y, oc, x)

    def to_z(step):
        return dev(wrap(z + step, Z), y, c, x)

    def to_y(step):
        return dev(z, wrap(y + step, Y), c, x)

    G = CORES * X
    m = c * X + x

    def to_m(step):
        mm = wrap(m + step, G)
        return dev(z, y, lax.div(mm, X), lax.rem(mm, X))

    barrier = pltpu.get_barrier_semaphore()
    friends = [partner] + [dev(z, y, c, wrap(x + k, X)) for k in range(1, X)]
    friends += [to_y(1), to_y(-1), to_z(1), to_z(-1)]
    for friend in friends:
        pl.semaphore_signal(barrier, inc=1, device_id=friend, device_id_type=MESH)

    locals_ = []

    def local(src, dst):
        copy = pltpu.make_async_copy(src, dst, lsem.at[len(locals_)])
        copy.start()
        locals_.append(copy)
        return copy

    F = doc_grad.shape[1]
    half = F // 2
    quarter = half // 2
    wc = in_basis.shape[1] // CORES
    nf = in_basis.shape[0]

    l_gq = local(query_grad.at[:, ds(c, half)], gq_own)
    l_inq = local(query_in, inq.at[:, ds(c, nf)])
    l_inb = local(in_basis.at[:, ds(c, wc)], inb.at[ds(c, nf), :])
    l_ind = local(doc_in, ind.at[:, ds(c, nf)])
    l_gd = local(doc_grad.at[:, ds(c, half)], gd_own)
    cols = out_basis.shape[0]
    theirs, ours = bb.at[0:cols, :], bb.at[cols : 2 * cols, :]
    l_b = local(out_basis.at[:, ds(c, half)], ours)
    l_eig = local(eigvals, eig)

    pl.semaphore_wait(barrier, len(friends))

    sent = []

    def send(src, dst, to):
        i = len(sent)
        copy = pltpu.make_async_remote_copy(
            src_ref=src, dst_ref=dst, send_sem=ssem.at[i], recv_sem=rsem.at[i], device_id=to, device_id_type=MESH
        )
        copy.start()
        sent.append(copy)
        return copy

    r_gq = send(query_grad.at[:, ds(oc, half)], gq_oth, partner)
    r_inq = send(query_in, inq.at[:, ds(c, nf)], partner)
    r_inb = send(in_basis.at[:, ds(oc, wc)], inb.at[ds(c, nf), :], partner)
    r_ind = send(doc_in, ind.at[:, ds(c, nf)], partner)
    r_gd = send(doc_grad.at[:, ds(oc, half)], gd_oth, partner)
    r_b = send(out_basis.at[:, ds(oc, half)], theirs, partner)

    def ring_ag(n, blk, there, to):
        h = n // 2

        def forward(o, step, b):
            return send(blk(o, b), there(o, step, b), to(step))

        r, l = forward(0, 1, None), forward(0, -1, None)
        for s in range(1, h):
            yield
            r.wait_recv()
            r = forward(-s, 1, None if s < h - 1 else 0)
            l.wait_recv()
            l = forward(s, -1, None if s < h - 1 else 1)
        yield
        r.wait_recv()
        l.wait_recv()

    def ring_rs(p, n, own_part, snd, rcv, width, to, done):
        h = n // 2
        lo, hi = slice(0, width // 2), slice(width // 2, width)
        r_half, l_half = rcv.at[0, 0, :, lo], rcv.at[1, 0, :, hi]
        snd[0, 0] = own_part(wrap(p + h, n)).astype(snd.dtype)
        r = send(snd.at[0, 0, :, lo], r_half, to(1))
        l = send(snd.at[0, 0, :, hi], l_half, to(-1))
        for s in range(1, h):
            yield
            own = own_part(wrap(p + h - s, n))
            r.wait_recv()
            if s == 1:
                snd[0, s, :, lo] = (own[:, lo] + rcv[0, 0, :, lo].astype(F32)).astype(snd.dtype)
                snd[0, s, :, hi] = own[:, hi].astype(snd.dtype)
            else:
                snd[0, s] = (own + rcv[0, s - 1].astype(F32)).astype(snd.dtype)
            r = send(snd.at[0, s], rcv.at[0, s], to(1))
            own = own_part(wrap(p - h + s, n))
            l.wait_recv()
            if s == 1:
                snd[1, s, :, lo] = own[:, lo].astype(snd.dtype)
                snd[1, s, :, hi] = (own[:, hi] + rcv[1, 0, :, hi].astype(F32)).astype(snd.dtype)
            else:
                snd[1, s] = (own + rcv[1, s - 1].astype(F32)).astype(snd.dtype)
            l = send(snd.at[1, s], rcv.at[1, s], to(-1))
        yield
        own = own_part(p)
        r.wait_recv()
        l.wait_recv()
        done(own + rcv[0, h - 1].astype(F32) + rcv[1, h - 1].astype(F32))

    rows_d = 2 * doc_grad.shape[0]

    shifted = min(SHIFTED, quarter)
    main = half - shifted

    def span(first, size, b):
        return pl.ds(first, size) if b is None else pl.ds(first + b * (size // 2), size // 2)

    def gd_rows(oz, yy):
        return pl.ds(pl.multiple_of((oz % Z) * Y * rows_d + yy * rows_d, rows_d), rows_d)

    def gd_blk(oz, yy, b=None):
        return gd.at[gd_rows(oz, yy), span(0, main, b)]

    def shift_task():
        def along(o, b):
            return gd.at[gd_rows(0, wrap(y + o, Y)), span(main, shifted, b)]

        def group(oz, b):
            return gd.at[pl.ds((oz % Z) * Y * rows_d, Y * rows_d), span(main, shifted, b)]

        yield from ring_ag(Y, along, lambda o, step, b: along(o, b), to_y)
        yield from ring_ag(Z, group, lambda o, step, b: group(o - step, b), to_z)

    def gq_blk(oz, yy, b=None):
        at = wrap(z + oz, Z) * Y + yy
        return gq.at[at] if b is None else gq.at[at, :, pl.ds(b * (quarter // 2), quarter // 2)]

    def along_y(blk, oz):
        def place(o, b):
            return blk(oz, wrap(y + o, Y), b)

        return ring_ag(Y, place, lambda o, step, b: place(o, b), to_y)

    tasks = {}
    for oz in range(Z):
        tasks["yq%d" % oz] = along_y(gq_blk, oz)
        tasks["yd%d" % oz] = along_y(gd_blk, oz)

    nq = query_grad.shape[0]
    first = c == 0
    l_gq.wait()
    r_gq.wait_recv()
    own, oth = gq_own[...].astype(F32), gq_oth[...].astype(F32)
    gq_f[0:nq, :] = jnp.where(first, own, oth)
    gq_f[nq : 2 * nq, :] = jnp.where(first, oth, own)
    gq[z * Y + y] = jnp.concatenate([gq_f[:, 0:quarter], gq_f[:, quarter:half]], axis=0).astype(BF16)
    ag_q = ring_ag(Z, lambda o, b: gq_blk(o, y, b), lambda o, step, b: gq_blk(o, y, b), to_z)
    tasks["q"] = ag_q
    next(ag_q)
    next(tasks["yq0"])

    dq, dd = query_in.shape[0], doc_in.shape[0]
    bq, bd = dq // Z, dd // Z
    wy = wc // Y
    for copy in (l_inq, l_inb):
        copy.wait()
    for copy in (r_inq, r_inb):
        copy.wait_recv()
    pin_q[...] = jnp.dot(inq[...], inb[...], preferred_element_type=F32)

    def in_task(pin, zs, zr, yr, rot, rows, place, rest):
        def put(v):
            for k in range(Y):
                yr[Y + k] = v[:, k * wy : (k + 1) * wy]

        yield from ring_rs(z, Z, lambda k: pin[ds(k, rows), :], zs, zr, wc, to_z, put)
        copies = [send(yr.at[Y + wrap(y + k, Y)], yr.at[y], to_y(k)) for k in range(1, Y)]
        yr[y] = yr[Y + y]
        yield
        for copy in copies:
            copy.wait_recv()
        total = yr[0]
        for k in range(1, Y):
            total = total + yr[k]
        mine = rot.at[place(0), ds(c * Y + y, wy)]
        mine[...] = total.astype(BF16)
        copies = [send(mine, mine, to_y(k)) for k in range(1, Y)]
        yield
        for copy in copies:
            copy.wait_recv()

        for name in rest:
            next(tasks[name])
        yield from spread(rot, place, 0, len(rest) + 1)

    def spread(rot, place, i, parts):
        size = wc // parts

        def cols_of(b):
            first, width = (c * parts + i, size) if b is None else ((c * parts + i) * 2 + b, size // 2)
            return ds(first, width)

        yield from ring_ag(
            Z, lambda o, b: rot.at[place(o), cols_of(b)], lambda o, step, b: rot.at[place(o, step), cols_of(b)], to_z
        )
        part = rot.at[:, cols_of(None)]
        copy = send(part, part, partner)
        yield
        copy.wait_recv()

    def place_q(o, step=0):
        return ds(wrap(z + o, Z), bq)

    def place_d(o, step=0):
        return pl.ds(((o - step) % Z) * bd, bd)

    in_q = in_task(pin_q, zs_q, zr_q, yr_q, rot_q, bq, place_q, ())
    in_d = in_task(pin_d, zs_d, zr_d, yr_d, rot_d, bd, place_d, ("E",))
    tasks["E"] = spread(rot_d, place_d, 1, 2)
    next(in_q)
    l_ind.wait()
    r_ind.wait_recv()
    pin_d[...] = jnp.dot(ind[...], inb[...], preferred_element_type=F32)
    next(in_d)

    l_gd.wait()
    r_gd.wait_recv()
    own, oth = gd_own[...].astype(F32), gd_oth[...].astype(F32)
    gd[ds(y, rows_d), :] = jnp.concatenate(
        [jnp.where(first, own, oth), jnp.where(first, oth, own)], axis=0
    ).astype(BF16)
    ag_d = ring_ag(Z, lambda o, b: gd_blk(o, y, b), lambda o, step, b: gd_blk(o - step, y, b), to_z)
    tasks.update(d=ag_d, x=shift_task(), Q=in_q, D=in_d)

    def matmul(a, b, out, at, tile):
        depth = a.shape[1]
        tile = math.gcd(depth, tile)
        contract = (((1,), (1,)), ((), ()))
        out[:, at] = lax.dot_general(a[:, 0:tile], b[:, 0:tile], contract, preferred_element_type=F32)

        def body(k, _):
            out[:, at] += lax.dot_general(a[:, ds(k, tile)], b[:, ds(k, tile)], contract, preferred_element_type=F32)
            return 0

        lax.fori_loop(1, depth // tile, body, 0)

    share = cols // X

    def out_task(grads, at):
        matmul(bb, grads, part, at, 896)
        swap = send(part.at[0:cols, at], p_rcv.at[:, at], partner)
        yield
        swap.wait_recv()
        x_snd[:, at] = (part[cols : 2 * cols, at] + p_rcv[:, at]).astype(X_DT)
        copies = []
        for k in range(1, X):
            to = wrap(x + k, X)
            copies.append(send(x_snd.at[ds(to, share), at], x_rcv.at[x, :, at], dev(z, y, c, to)))
        yield
        for copy in copies:
            copy.wait_recv()
        mine = ds(x, share)
        x_rcv[x, :, at] = x_snd[mine, at]
        total = x_rcv[0, :, at].astype(F32)
        for k in range(1, X):
            total = total + x_rcv[k, :, at].astype(F32)
        out_rot[mine, at] = total.astype(BF16)
        copies = []
        for k in range(1, X):
            copies.append(send(out_rot.at[mine, at], out_rot.at[mine, at], dev(z, y, c, wrap(x + k, X))))
        yield
        for copy in copies:
            copy.wait_recv()

    def out_queries():
        l_b.wait()
        r_b.wait_recv()
        rows = gq.shape[1] // 2
        for h in range(2):
            gq2[:, h * quarter : (h + 1) * quarter] = (
                gq[:, h * rows : (h + 1) * rows, :].astype(F32).reshape(dq, quarter).astype(BF16)
            )
        yield from out_task(gq2, slice(0, dq))

    chunk = 2 * (dd // Z)
    tasks["oq"] = out_queries()
    for i in range(Z // 2):
        tasks["o%d" % i] = out_task(
            gd.at[i * chunk : (i + 1) * chunk, :], slice(dq + i * chunk, dq + (i + 1) * chunk)
        )

    tile = 256
    n_tiles = eig.shape[1] // tile

    def precondition(i):
        at = ds(i, tile)
        factor = eig[:, at]
        grad = jnp.dot(mq[...], rot_q[:, at], preferred_element_type=F32)
        total = None
        for q in range(QUERIES):
            block = (grad[q * cols : (q + 1) * cols] * factor).astype(BF16)
            prec[q * cols : (q + 1) * cols, at] = block
            block = block.astype(F32)
            total = block if total is None else total + block
        ihvp[:, at] = total.astype(BF16)

    def factors():
        yield
        l_eig.wait()
        for i in range(n_tiles):
            if i:
                yield
            at = ds(i, tile)
            eig[:, at] = math.sqrt(dq) / (eig[:, at] + DAMPING)

    def precondition_all():
        yield
        ids_q = query_ids[...]
        for q in range(QUERIES):
            mq[q * cols : (q + 1) * cols, :] = jnp.where(ids_q == q, out_rot[:, 0:dq].astype(F32), 0.0).astype(BF16)
        for i in range(n_tiles):
            if i:
                yield
            precondition(i)

    def project(i):
        size = wc // 2
        for core in range(CORES):
            yield
            at = slice(core * wc + i * size, core * wc + (i + 1) * size)
            block = lax.dot_general(
                prec[:, at], rot_d[:, at], (((1,), (1,)), ((), ())), preferred_element_type=F32
            )
            proj[...] = block if i + core == 0 else proj[...] + block

    tasks.update(F=factors(), P=precondition_all(), R=project(0), S=project(1))
    for name in PLAN:
        next(tasks[name], None)
    for task in tasks.values():
        for _ in task:
            pass

    ids_d = pltpu.roll(jnp.broadcast_to(doc_ids[...], (8, dd)), dd - z * (dd // Z), 1)
    hot = ids_d == lax.broadcasted_iota(jnp.int32, (8, dd), 0)
    row_id = lax.broadcasted_iota(jnp.int32, (8, 128), 0)
    lane_id = lax.broadcasted_iota(jnp.int32, (8, 128), 1)
    value = jnp.zeros((8, 128), F32)
    for q in range(QUERIES):
        token = jnp.sum(
            proj[q * cols : (q + 1) * cols, :] * out_rot[:, dq : dq + dd].astype(F32), axis=0, keepdims=True
        )
        per_doc = jnp.sum(jnp.where(hot, token, 0.0), axis=1, keepdims=True)
        for d in range(DOCS):
            value = jnp.where((row_id == q) & (lane_id == d), per_doc[d : d + 1, :], value)

    def exchange(buf, me, n, to, value):
        buf[me] = value
        copies = [send(buf.at[me], buf.at[me], to(k)) for k in range(1, n)]
        for copy in copies:
            copy.wait_recv()
        return jnp.sum(buf[...], axis=0)

    value = exchange(sc_a, m, G, to_m, value)
    value = exchange(sc_b, y, Y, to_y, value)
    value = exchange(sc_c, z, Z, to_z, value)
    scores[...] = value[0:QUERIES, 0:DOCS] * scale

    for copy in sent:
        copy.wait_send()


def shards(
    Z, X, doc_in, query_in, doc_grad, query_grad, doc_ids, query_ids, in_basis, out_basis, eigvals
):
    dd, dq = doc_in.shape[0], query_in.shape[0]
    out_basis = out_basis.T
    cols, F = out_basis.shape
    half, quarter = F // 2, F // 4
    nf, width = in_basis.shape
    wc = width // CORES
    wy = wc // Y
    bq, bd = dq // Z, dd // Z
    hz = Z // 2
    n_docs, n_q = doc_grad.shape[0], query_grad.shape[0]
    scale = 1.0 / math.sqrt(width * X * cols * Z * Y * CORES * dd)
    vmem = pltpu.VMEM
    any_ = pl.BlockSpec(memory_space=pl.ANY)
    in_vmem = pl.BlockSpec(memory_space=pltpu.VMEM)
    ihvp, scores = pl.pallas_call(
        functools.partial(kernel, Z, X, scale),
        out_shape=(
            pltpu.VMEM((cols, width), BF16),
            jax.ShapeDtypeStruct((QUERIES, DOCS), F32),
        ),
        in_specs=[any_, any_, any_, any_, in_vmem, in_vmem, any_, any_, any_],
        out_specs=(in_vmem, in_vmem),
        scratch_shapes=[
            vmem((dq, CORES * nf), BF16), vmem((dd, CORES * nf), BF16), vmem((CORES * nf, wc), BF16),
            vmem((n_docs, half), BF16), vmem((n_docs, half), BF16),
            vmem((n_q, half), BF16), vmem((n_q, half), BF16), vmem((2 * n_q, half), F32),
            vmem((dd, half), BF16), vmem((Z * Y, 4 * n_q, quarter), BF16), vmem((dq, half), BF16),
            vmem((2 * cols, half), BF16), vmem((cols, width), F32),
            vmem((dq, wc), F32), vmem((dd, wc), F32),
            vmem((2, hz, bq, wc), RS_DT), vmem((2, hz, bq, wc), RS_DT),
            vmem((2, hz, bd, wc), RS_DT), vmem((2, hz, bd, wc), RS_DT),
            vmem((2 * Y, bq, wy), F32), vmem((2 * Y, bd, wy), F32),
            vmem((dq, width), BF16), vmem((dd, width), BF16),
            vmem((2 * cols, dq + dd), F32), vmem((cols, dq + dd), F32),
            vmem((cols, dq + dd), X_DT), vmem((X, cols // X, dq + dd), X_DT), vmem((cols, dq + dd), BF16),
            vmem((QUERIES * cols, dq), BF16), vmem((QUERIES * cols, width), BF16),
            vmem((QUERIES * cols, dd), F32),
            vmem((CORES * X, 8, 128), F32), vmem((Y, 8, 128), F32), vmem((Z, 8, 128), F32),
            pltpu.SemaphoreType.DMA((N_SEM,)), pltpu.SemaphoreType.DMA((N_SEM,)), pltpu.SemaphoreType.DMA((32,)),
        ],
        compiler_params=pltpu.CompilerParams(
            collective_id=0, has_side_effects=True, vmem_limit_bytes=62 * 1024 * 1024
        ),
    )(
        doc_in, query_in, doc_grad, query_grad, doc_ids.reshape(1, dd), query_ids.reshape(1, dq),
        in_basis, out_basis, eigvals.T,
    )
    return ihvp.T, scores


def solution(mesh):
    placed = (
        P(None, "tok"),
        P(None, "tok"),
        P("tok", "feat"),
        P("tok", "feat"),
        P(),
        P(),
        P("tok", "feat"),
        P("feat", "tok"),
        P("feat", "tok"),
    )
    X = mesh.shape["feat"]
    Z = mesh.shape["tok"] // (Y * CORES)
    return jax.shard_map(
        functools.partial(shards, Z, X), mesh=mesh, in_specs=placed, out_specs=(P("feat", "tok"), P()), check_vma=False
    )
```

```python
import functools
import math

import jax
import jax.numpy as jnp
from jax import lax
from jax.experimental import pallas as pl
from jax.experimental.pallas import tpu as pltpu
from jax.sharding import PartitionSpec as P

DOCS = 4
QUERIES = 2
DAMPING = 0.1
Y = 4
CORES = 2
RS_DT = jnp.bfloat16
X_DT = jnp.bfloat16
F32 = jnp.float32
BF16 = jnp.bfloat16
MESH = pl.DeviceIdType.MESH
N_SEM = 256
IN_FLIGHT = 48
SHIFTED = 1024
PLAN = (
    "yd0", "yq0", "q", "yq1", "yq7", "Q", "x", "D", "yd0", "F", "F", "F", "F", "q", "yq0", "yq2", "F", "F", "yq1",
    "Q", "F", "F", "x", "yq7", "F", "D", "yd0", "yq6", "q", "yq2", "x", "yq1", "yq3", "Q", "yq7", "yq5", "yq6", "d",
    "yq2", "D", "q", "yq4", "yq3", "x", "yq5", "yq6", "yq4", "Q", "d", "yd1", "yq3", "yd7", "yq5", "yq4", "oq", "Q",
    "D", "yd1", "x", "oq", "yd7", "d", "yd2", "yd6", "Q", "x", "D", "yd1", "d", "yd7", "yd3", "yd2", "oq", "Q", "x",
    "o0", "d", "yd6", "D", "Q", "o0", "yd5", "oq", "yd3", "yd2", "yd4", "E", "yd6", "o3", "D", "yd5", "o0", "yd3",
    "o1", "o3", "yd4", "E", "Q", "yd5", "D", "o0", "o1", "yd4", "o2", "E", "o3", "Q", "D", "o2", "o1", "E", "Q",
    "P", "P", "P", "P", "P", "o3", "D", "P", "P", "E", "P", "P", "o2", "D", "R", "R", "R", "S", "o1", "S", "S", "o2",
)


def ds(i, size):
    return pl.ds(pl.multiple_of(i * size, size), size)


def kernel(
    Z, X, scale,
    doc_in, query_in, doc_grad, query_grad, doc_ids, query_ids, in_basis, out_basis, eigvals,
    ihvp, scores,
    inq, ind, inb, gd_own, gd_oth, gq_own, gq_oth, gq_f, gd, gq, gq2, bb, eig,
    pin_q, pin_d, zs_q, zr_q, zs_d, zr_d, yr_q, yr_d, rot_q, rot_d,
    part, p_rcv, xs_q, xr_q, xs_d, xr_d, out_rot, mq, prec, proj, sc_a, sc_b, sc_c,
    ssem, rsem, lsem,
):
    tok, x = lax.axis_index("tok"), lax.axis_index("feat")
    c = lax.rem(tok, CORES)
    y = lax.rem(lax.div(tok, CORES), Y)
    z = lax.div(tok, CORES * Y)
    oc = 1 - c

    def dev(zz, yy, cc, xx):
        return ((zz * Y + yy) * CORES + cc, xx)

    def wrap(v, n):
        return lax.rem(v + 4 * n, n)

    partner = dev(z, y, oc, x)

    def to_z(step):
        return dev(wrap(z + step, Z), y, c, x)

    def to_y(step):
        return dev(z, wrap(y + step, Y), c, x)

    G = CORES * X
    m = c * X + x

    def to_m(step):
        mm = wrap(m + step, G)
        return dev(z, y, lax.div(mm, X), lax.rem(mm, X))

    barrier = pltpu.get_barrier_semaphore()
    friends = [partner] + [dev(z, y, c, wrap(x + k, X)) for k in range(1, X)]
    friends += [to_y(1), to_y(-1), to_z(1), to_z(-1)]
    for friend in friends:
        pl.semaphore_signal(barrier, inc=1, device_id=friend, device_id_type=MESH)

    locals_ = []

    def local(src, dst):
        copy = pltpu.make_async_copy(src, dst, lsem.at[len(locals_)])
        copy.start()
        locals_.append(copy)
        return copy

    F = doc_grad.shape[1]
    half = F // 2
    quarter = half // 2
    wc = in_basis.shape[1] // CORES
    nf = in_basis.shape[0]

    l_gq = local(query_grad.at[:, ds(c, half)], gq_own)
    l_inq = local(query_in, inq.at[:, ds(c, nf)])
    l_inb = local(in_basis.at[:, ds(c, wc)], inb.at[ds(c, nf), :])
    l_ind = local(doc_in, ind.at[:, ds(c, nf)])
    l_gd = local(doc_grad.at[:, ds(c, half)], gd_own)
    cols = out_basis.shape[0]
    theirs, ours = bb.at[0:cols, :], bb.at[cols : 2 * cols, :]
    l_b = local(out_basis.at[:, ds(c, half)], ours)
    l_eig = local(eigvals, eig)

    pl.semaphore_wait(barrier, len(friends))

    sent = []

    def send(src, dst, to):
        i = len(sent)
        copy = pltpu.make_async_remote_copy(
            src_ref=src, dst_ref=dst, send_sem=ssem.at[i], recv_sem=rsem.at[i], device_id=to, device_id_type=MESH
        )
        copy.start()
        sent.append(copy)
        return copy

    settled = []

    def settle(few):
        while len(settled) < len(sent) - few:
            copy = sent[len(settled)]
            copy.wait_send()
            settled.append(copy)

    r_gq = send(query_grad.at[:, ds(oc, half)], gq_oth, partner)
    r_inq = send(query_in, inq.at[:, ds(c, nf)], partner)
    r_inb = send(in_basis.at[:, ds(oc, wc)], inb.at[ds(c, nf), :], partner)
    r_ind = send(doc_in, ind.at[:, ds(c, nf)], partner)
    r_gd = send(doc_grad.at[:, ds(oc, half)], gd_oth, partner)
    r_b = send(out_basis.at[:, ds(oc, half)], theirs, partner)

    def ring_ag(n, blk, there, to):
        h = n // 2

        def forward(o, step, b):
            return send(blk(o, b), there(o, step, b), to(step))

        r, l = forward(0, 1, None), forward(0, -1, None)
        for s in range(1, h):
            yield
            r.wait_recv()
            r = forward(-s, 1, None if s < h - 1 else 0)
            l.wait_recv()
            l = forward(s, -1, None if s < h - 1 else 1)
        yield
        r.wait_recv()
        l.wait_recv()

    def ring_rs(p, n, own_part, snd, rcv, width, to, done):
        h = n // 2
        lo, hi = slice(0, width // 2), slice(width // 2, width)
        r_half, l_half = rcv.at[0, 0, :, lo], rcv.at[1, 0, :, hi]
        snd[0, 0] = own_part(wrap(p + h, n)).astype(snd.dtype)
        r = send(snd.at[0, 0, :, lo], r_half, to(1))
        l = send(snd.at[0, 0, :, hi], l_half, to(-1))
        for s in range(1, h):
            yield
            own = own_part(wrap(p + h - s, n))
            r.wait_recv()
            if s == 1:
                snd[0, s, :, lo] = (own[:, lo] + rcv[0, 0, :, lo].astype(F32)).astype(snd.dtype)
                snd[0, s, :, hi] = own[:, hi].astype(snd.dtype)
            else:
                snd[0, s] = (own + rcv[0, s - 1].astype(F32)).astype(snd.dtype)
            r = send(snd.at[0, s], rcv.at[0, s], to(1))
            own = own_part(wrap(p - h + s, n))
            l.wait_recv()
            if s == 1:
                snd[1, s, :, lo] = own[:, lo].astype(snd.dtype)
                snd[1, s, :, hi] = (own[:, hi] + rcv[1, 0, :, hi].astype(F32)).astype(snd.dtype)
            else:
                snd[1, s] = (own + rcv[1, s - 1].astype(F32)).astype(snd.dtype)
            l = send(snd.at[1, s], rcv.at[1, s], to(-1))
        yield
        own = own_part(p)
        r.wait_recv()
        l.wait_recv()
        done(own + rcv[0, h - 1].astype(F32) + rcv[1, h - 1].astype(F32))

    rows_d = 2 * doc_grad.shape[0]

    shifted = min(SHIFTED, quarter)
    main = half - shifted

    def span(first, size, b):
        return pl.ds(first, size) if b is None else pl.ds(first + b * (size // 2), size // 2)

    def gd_rows(oz, yy):
        return pl.ds(pl.multiple_of((oz % Z) * Y * rows_d + yy * rows_d, rows_d), rows_d)

    def gd_blk(oz, yy, b=None):
        return gd.at[gd_rows(oz, yy), span(0, main, b)]

    def shift_task():
        def along(o, b):
            return gd.at[gd_rows(0, wrap(y + o, Y)), span(main, shifted, b)]

        def group(oz, b):
            return gd.at[pl.ds((oz % Z) * Y * rows_d, Y * rows_d), span(main, shifted, b)]

        yield from ring_ag(Y, along, lambda o, step, b: along(o, b), to_y)
        yield from ring_ag(Z, group, lambda o, step, b: group(o - step, b), to_z)

    def gq_blk(oz, yy, b=None):
        at = wrap(z + oz, Z) * Y + yy
        return gq.at[at] if b is None else gq.at[at, :, pl.ds(b * (quarter // 2), quarter // 2)]

    def along_y(blk, oz):
        def place(o, b):
            return blk(oz, wrap(y + o, Y), b)

        return ring_ag(Y, place, lambda o, step, b: place(o, b), to_y)

    tasks = {}
    for oz in range(Z):
        tasks["yq%d" % oz] = along_y(gq_blk, oz)
        tasks["yd%d" % oz] = along_y(gd_blk, oz)

    nq = query_grad.shape[0]
    first = c == 0
    l_gq.wait()
    r_gq.wait_recv()
    own, oth = gq_own[...].astype(F32), gq_oth[...].astype(F32)
    gq_f[0:nq, :] = jnp.where(first, own, oth)
    gq_f[nq : 2 * nq, :] = jnp.where(first, oth, own)
    gq[z * Y + y] = jnp.concatenate([gq_f[:, 0:quarter], gq_f[:, quarter:half]], axis=0).astype(BF16)
    ag_q = ring_ag(Z, lambda o, b: gq_blk(o, y, b), lambda o, step, b: gq_blk(o, y, b), to_z)
    tasks["q"] = ag_q
    next(ag_q)
    next(tasks["yq0"])

    dq, dd = query_in.shape[0], doc_in.shape[0]
    bq, bd = dq // Z, dd // Z
    wy = wc // Y
    for copy in (l_inq, l_inb):
        copy.wait()
    for copy in (r_inq, r_inb):
        copy.wait_recv()
    pin_q[...] = jnp.dot(inq[...], inb[...], preferred_element_type=F32)

    def in_task(pin, zs, zr, yr, rot, rows, place, rest):
        def put(v):
            for k in range(Y):
                yr[Y + k] = v[:, k * wy : (k + 1) * wy]

        yield from ring_rs(z, Z, lambda k: pin[ds(k, rows), :], zs, zr, wc, to_z, put)
        copies = [send(yr.at[Y + wrap(y + k, Y)], yr.at[y], to_y(k)) for k in range(1, Y)]
        yr[y] = yr[Y + y]
        yield
        for copy in copies:
            copy.wait_recv()
        total = yr[0]
        for k in range(1, Y):
            total = total + yr[k]
        mine = rot.at[place(0), ds(c * Y + y, wy)]
        mine[...] = total.astype(BF16)
        copies = [send(mine, mine, to_y(k)) for k in range(1, Y)]
        yield
        for copy in copies:
            copy.wait_recv()

        for name in rest:
            next(tasks[name])
        yield from spread(rot, place, 0, len(rest) + 1)

    def spread(rot, place, i, parts):
        size = wc // parts

        def cols_of(b):
            first, width = (c * parts + i, size) if b is None else ((c * parts + i) * 2 + b, size // 2)
            return ds(first, width)

        yield from ring_ag(
            Z, lambda o, b: rot.at[place(o), cols_of(b)], lambda o, step, b: rot.at[place(o, step), cols_of(b)], to_z
        )
        part = rot.at[:, cols_of(None)]
        copy = send(part, part, partner)
        yield
        copy.wait_recv()

    def place_q(o, step=0):
        return ds(wrap(z + o, Z), bq)

    def place_d(o, step=0):
        return pl.ds(((o - step) % Z) * bd, bd)

    in_q = in_task(pin_q, zs_q, zr_q, yr_q, rot_q, bq, place_q, ())
    in_d = in_task(pin_d, zs_d, zr_d, yr_d, rot_d, bd, place_d, ("E",))
    tasks["E"] = spread(rot_d, place_d, 1, 2)
    next(in_q)
    l_ind.wait()
    r_ind.wait_recv()
    pin_d[...] = jnp.dot(ind[...], inb[...], preferred_element_type=F32)
    next(in_d)

    l_gd.wait()
    r_gd.wait_recv()
    own, oth = gd_own[...].astype(F32), gd_oth[...].astype(F32)
    gd[ds(y, rows_d), :] = jnp.concatenate(
        [jnp.where(first, own, oth), jnp.where(first, oth, own)], axis=0
    ).astype(BF16)
    ag_d = ring_ag(Z, lambda o, b: gd_blk(o, y, b), lambda o, step, b: gd_blk(o - step, y, b), to_z)
    tasks.update(d=ag_d, x=shift_task(), Q=in_q, D=in_d)

    def matmul(a, b, out, at, tile):
        depth = a.shape[1]
        tile = math.gcd(depth, tile)
        contract = (((1,), (1,)), ((), ()))
        out[:, at] = lax.dot_general(a[:, 0:tile], b[:, 0:tile], contract, preferred_element_type=F32)

        def body(k, _):
            out[:, at] += lax.dot_general(a[:, ds(k, tile)], b[:, ds(k, tile)], contract, preferred_element_type=F32)
            return 0

        lax.fori_loop(1, depth // tile, body, 0)

    share = cols // X

    def out_task(grads, at, snd, rcv, own):
        matmul(bb, grads, part, at, 896)
        swap = send(part.at[0:cols, at], p_rcv.at[:, at], partner)
        yield
        swap.wait_recv()
        total = part[cols : 2 * cols, at] + p_rcv[:, at]
        p_rcv[:, at] = total
        snd[:, own] = total.astype(snd.dtype)
        copies = []
        for k in range(1, X):
            to = wrap(x + k, X)
            copies.append(send(snd.at[ds(to, share), own], rcv.at[x, :, own], dev(z, y, c, to)))
        yield
        for copy in copies:
            copy.wait_recv()
        mine = ds(x, share)
        total = p_rcv[mine, at]
        for k in range(1, X):
            total = total + rcv[wrap(x + k, X), :, own].astype(F32)
        out_rot[mine, at] = total.astype(BF16)
        copies = []
        for k in range(1, X):
            copies.append(send(out_rot.at[mine, at], out_rot.at[mine, at], dev(z, y, c, wrap(x + k, X))))
        yield
        for copy in copies:
            copy.wait_recv()

    def out_queries():
        l_b.wait()
        r_b.wait_recv()
        rows = gq.shape[1] // 2
        for h in range(2):
            gq2[:, h * quarter : (h + 1) * quarter] = (
                gq[:, h * rows : (h + 1) * rows, :].astype(F32).reshape(dq, quarter).astype(BF16)
            )
        yield from out_task(gq2, slice(0, dq), xs_q, xr_q, slice(0, dq))

    chunk = 2 * (dd // Z)
    tasks["oq"] = out_queries()
    for i in range(Z // 2):
        own = slice(i * chunk, (i + 1) * chunk)
        tasks["o%d" % i] = out_task(gd.at[own, :], slice(dq + own.start, dq + own.stop), xs_d, xr_d, own)

    tile = 256
    n_tiles = eig.shape[1] // tile

    def precondition(i):
        at = ds(i, tile)
        factor = eig[:, at]
        grad = jnp.dot(mq[...], rot_q[:, at], preferred_element_type=F32)
        total = None
        for q in range(QUERIES):
            block = (grad[q * cols : (q + 1) * cols] * factor).astype(BF16)
            prec[q * cols : (q + 1) * cols, at] = block
            block = block.astype(F32)
            total = block if total is None else total + block
        ihvp[:, at] = total.astype(BF16)

    def factors():
        yield
        l_eig.wait()
        for i in range(n_tiles):
            if i:
                yield
            at = ds(i, tile)
            eig[:, at] = math.sqrt(dq) / (eig[:, at] + DAMPING)

    def precondition_all():
        yield
        ids_q = query_ids[...]
        for q in range(QUERIES):
            mq[q * cols : (q + 1) * cols, :] = jnp.where(ids_q == q, out_rot[:, 0:dq].astype(F32), 0.0).astype(BF16)
        for i in range(n_tiles):
            if i:
                yield
            precondition(i)

    def project(i):
        size = wc // 2
        for core in range(CORES):
            yield
            at = slice(core * wc + i * size, core * wc + (i + 1) * size)
            block = lax.dot_general(
                prec[:, at], rot_d[:, at], (((1,), (1,)), ((), ())), preferred_element_type=F32
            )
            proj[...] = block if i + core == 0 else proj[...] + block

    tasks.update(F=factors(), P=precondition_all(), R=project(0), S=project(1))
    for name in PLAN:
        next(tasks[name], None)
        settle(IN_FLIGHT)
    for task in tasks.values():
        for _ in task:
            pass

    ids_d = pltpu.roll(jnp.broadcast_to(doc_ids[...], (8, dd)), dd - z * (dd // Z), 1)
    hot = ids_d == lax.broadcasted_iota(jnp.int32, (8, dd), 0)
    row_id = lax.broadcasted_iota(jnp.int32, (8, 128), 0)
    lane_id = lax.broadcasted_iota(jnp.int32, (8, 128), 1)
    value = jnp.zeros((8, 128), F32)
    for q in range(QUERIES):
        token = jnp.sum(
            proj[q * cols : (q + 1) * cols, :] * out_rot[:, dq : dq + dd].astype(F32), axis=0, keepdims=True
        )
        per_doc = jnp.sum(jnp.where(hot, token, 0.0), axis=1, keepdims=True)
        for d in range(DOCS):
            value = jnp.where((row_id == q) & (lane_id == d), per_doc[d : d + 1, :], value)

    def exchange(buf, me, n, to, value):
        buf[me] = value
        copies = [send(buf.at[me], buf.at[me], to(k)) for k in range(1, n)]
        settle(n - 1)
        for copy in copies:
            copy.wait_recv()
        return jnp.sum(buf[...], axis=0)

    value = exchange(sc_a, m, G, to_m, value)
    value = exchange(sc_b, y, Y, to_y, value)
    value = exchange(sc_c, z, Z, to_z, value)
    scores[...] = value[0:QUERIES, 0:DOCS] * scale

    settle(0)


def shards(
    Z, X, doc_in, query_in, doc_grad, query_grad, doc_ids, query_ids, in_basis, out_basis, eigvals
):
    dd, dq = doc_in.shape[0], query_in.shape[0]
    out_basis = out_basis.T
    cols, F = out_basis.shape
    half, quarter = F // 2, F // 4
    nf, width = in_basis.shape
    wc = width // CORES
    wy = wc // Y
    bq, bd = dq // Z, dd // Z
    hz = Z // 2
    n_docs, n_q = doc_grad.shape[0], query_grad.shape[0]
    scale = 1.0 / math.sqrt(width * X * cols * Z * Y * CORES * dd)
    vmem = pltpu.VMEM
    any_ = pl.BlockSpec(memory_space=pl.ANY)
    in_vmem = pl.BlockSpec(memory_space=pltpu.VMEM)
    ihvp, scores = pl.pallas_call(
        functools.partial(kernel, Z, X, scale),
        out_shape=(
            pltpu.VMEM((cols, width), BF16),
            jax.ShapeDtypeStruct((QUERIES, DOCS), F32),
        ),
        in_specs=[any_, any_, any_, any_, in_vmem, in_vmem, any_, any_, any_],
        out_specs=(in_vmem, in_vmem),
        scratch_shapes=[
            vmem((dq, CORES * nf), BF16), vmem((dd, CORES * nf), BF16), vmem((CORES * nf, wc), BF16),
            vmem((n_docs, half), BF16), vmem((n_docs, half), BF16),
            vmem((n_q, half), BF16), vmem((n_q, half), BF16), vmem((2 * n_q, half), F32),
            vmem((dd, half), BF16), vmem((Z * Y, 4 * n_q, quarter), BF16), vmem((dq, half), BF16),
            vmem((2 * cols, half), BF16), vmem((cols, width), F32),
            vmem((dq, wc), F32), vmem((dd, wc), F32),
            vmem((2, hz, bq, wc), RS_DT), vmem((2, hz, bq, wc), RS_DT),
            vmem((2, hz, bd, wc), RS_DT), vmem((2, hz, bd, wc), RS_DT),
            vmem((2 * Y, bq, wy), F32), vmem((2 * Y, bd, wy), F32),
            vmem((dq, width), BF16), vmem((dd, width), BF16),
            vmem((2 * cols, dq + dd), F32), vmem((cols, dq + dd), F32),
            vmem((cols, dq), F32), vmem((X, cols // X, dq), F32), vmem((cols, dd), X_DT), vmem((X, cols // X, dd), X_DT),
            vmem((cols, dq + dd), BF16),
            vmem((QUERIES * cols, dq), BF16), vmem((QUERIES * cols, width), BF16),
            vmem((QUERIES * cols, dd), F32),
            vmem((CORES * X, 8, 128), F32), vmem((Y, 8, 128), F32), vmem((Z, 8, 128), F32),
            pltpu.SemaphoreType.DMA((N_SEM,)), pltpu.SemaphoreType.DMA((N_SEM,)), pltpu.SemaphoreType.DMA((32,)),
        ],
        compiler_params=pltpu.CompilerParams(
            collective_id=0, has_side_effects=True, vmem_limit_bytes=62 * 1024 * 1024
        ),
    )(
        doc_in, query_in, doc_grad, query_grad, doc_ids.reshape(1, dd), query_ids.reshape(1, dq),
        in_basis, out_basis, eigvals.T,
    )
    return ihvp.T, scores


def solution(mesh):
    placed = (
        P(None, "tok"),
        P(None, "tok"),
        P("tok", "feat"),
        P("tok", "feat"),
        P(),
        P(),
        P("tok", "feat"),
        P("feat", "tok"),
        P("feat", "tok"),
    )
    X = mesh.shape["feat"]
    Z = mesh.shape["tok"] // (Y * CORES)
    return jax.shard_map(
        functools.partial(shards, Z, X), mesh=mesh, in_specs=placed, out_specs=(P("feat", "tok"), P()), check_vma=False
    )
```
